256 devices in a mesh: inst: 16 (over z_hi, y), ep: 16 (over x, z_lo, core).
Axes of the slice: x: 4, y: 4, z: 8 (z_hi: 4, z_lo: 2; z = z_hi * 2 + z_lo), core: 2. Of those that a mesh axis runs over, the one named last changes fastest.
Arguments:
- queries: bfloat16 [16, 16, 4, 8192], P('inst', 'ep'), may hold values from -120 to 120
- kv_cache: bfloat16 [16, 16, 2, 16, 64, 512], P('inst', 'ep'), may hold values from -6 to 6
- ctx_len: int32 [16, 16, 4], P('inst', 'ep'), may hold values from 1 to 512, 768 in all within a row
- page_order: int32 [16, 16, 16], P('inst', 'ep'), may hold values from 0 to 15, each once within a row
- hidden_in: bfloat16 [32768, 4096], P(('inst', 'ep')), may hold values from -6 to 6
- routes: int32 [32768, 1], P(('inst', 'ep')), may hold values from 0 to 3; in each aligned block of 128 rows (0 to 127, 128 to 255, ...) at most 64 rows name the same one
- w_gate: bfloat16 [16, 4096, 384], P('ep'), may hold values from -0.09375 to 0.09375
- w_up: bfloat16 [16, 4096, 384], P('ep'), may hold values from -0.09375 to 0.09375
- w_down: bfloat16 [16, 384, 4096], P('ep'), may hold values from -0.15625 to 0.15625
Outputs:
- attn_out: bfloat16 [16, 16, 4, 8192], P('inst', 'ep')
- moe_out: bfloat16 [32768, 4096], P(('inst', 'ep'))
- moved_pages: bfloat16 [16, 16, 2, 8, 64, 512], P('inst', 'ep')
The draws below stay inside these ranges and needn't reach their ends.
Inputs may be any that keep to these rules, and one draw needn't show every extreme that they name: `ctx_len`: the lengths of one device's requests sum to 768, and one of them is 512. `page_order`: each device's list holds each of its pages once. `routes`: the 128 tokens of one device name each expert at most 64 times, a bound that some block reaches.
All inputs are finite; a program needn't handle non-finite values.
Results may differ from the reference program's by a relative error of at most 0.011.
Values may be sent and summed in bfloat16 or wider, within the bound.
No kernel may reach another device: no remote copies, remote signals or barrier semaphores. Data moves between devices by JAX's collectives and lax.ppermute only.
A program may use at most 128 MiB of HBM per device.

```python
import math
import jax
import jax.numpy as jnp
import numpy as np
from jax import lax

D = 4096
HEADS = 64
KV_HEADS = 4
HEAD_DIM = 128
FF = 1536
FF_SPLIT = 4
TOP = 1
PAGE = 64
MAXP = 8
REQ_DEV = 4
TOK_DEV = 128
PAGES_DEV = 16
EXPERTS = 4
CAP = 64
N_INST = 16
N_EP = 16


def draw_kv_cache(key, part):
    key = jax.random.fold_in(key, 1)
    shape = (N_INST, N_EP, 2, PAGES_DEV, PAGE, KV_HEADS * HEAD_DIM)
    result = jnp.clip(jax.random.normal(key, shape, jnp.float32), -6.0, 6.0)
    return result.astype(jnp.bfloat16)


def draw_queries(key, part):
    key = jax.random.fold_in(key, 2)
    shape = (N_INST, N_EP, REQ_DEV, HEADS, HEAD_DIM)
    result = jnp.clip(jax.random.normal(key, shape, jnp.float32), -6.0, 6.0)
    return result.reshape(N_INST, N_EP, REQ_DEV, HEADS * HEAD_DIM).astype(jnp.bfloat16)


def level_of(own_key, extent, shards, least, high):
    factor_of = 1.0
    for position, blocks in shards:
        steps = jax.random.uniform(jax.random.fold_in(jax.random.fold_in(own_key, 6), position), (blocks,), jnp.float32, least / len(shards), high / len(shards))
        factor_of = factor_of * jnp.repeat(jnp.exp(steps), extent[position] // blocks).reshape((-1,) + (1,) * (len(extent) - 1 - position))
    return factor_of


def length_profile(count, total, bound, slope):
    weights = [(1 << 20) // math.isqrt(grade ** slope) + 1 for grade in range(2, count + 1)]
    surplus, given = total - bound - (count - 1), [1] * (count - 1)
    while surplus > 0:
        candidates = [i for i in range(count - 1) if given[i] < bound]
        mass, left = sum([weights[i] for i in candidates]), surplus
        for i in candidates:
            extra = min(bound - given[i], max(1, left * weights[i] // mass), surplus)
            given[i] = given[i] + extra
            surplus = surplus - extra
    return np.array([bound] + given)


def ragged(own_key, number_of, total, bound, slope):
    if number_of == 2:
        one = jax.random.randint(own_key, (), max(1, total - bound), min(bound, total - 1) + 1)
        return jnp.stack([one, total - one])
    tallies = jnp.asarray(length_profile(number_of, total, bound, slope), jnp.int32)
    couples = (number_of - 1) // 2
    giver, taker = tallies[1:1 + 2 * couples:2], tallies[2:2 + 2 * couples:2]
    slack = jnp.minimum(giver - 1, bound - taker)
    moved = jax.random.randint(jax.random.fold_in(own_key, 1), (couples,), 0, 1 << 20) % (slack + 1)
    tallies = tallies.at[1:1 + 2 * couples:2].set(giver - moved).at[2:2 + 2 * couples:2].set(taker + moved)
    return tallies[jax.random.permutation(jax.random.fold_in(own_key, 2), number_of)]


def deal_out(stream_key, own, number, rows, number_of, top, most, slope):
    order = jax.random.permutation(stream_key, number_of)
    crowded, ordinary = portions_of(number_of, rows * top, most, slope, True), portions_of(number_of, rows * top, most, slope, False)
    places = jnp.arange(number_of)

    def named(lengths, turn):
        used = int((lengths > 0).sum())
        fixed = max(1, used // 4)
        passed = fixed + (places - fixed + turn * (used - fixed)) % max(1, number_of - fixed)
        return jnp.zeros((number_of,), jnp.int32).at[order[jnp.where(places < fixed, places, passed)]].set(jnp.asarray(lengths, jnp.int32))

    lengths = jnp.where(number % 4 == 0, named(crowded, number // 4), named(ordinary, number - number // 4 - 1))
    mixed = jax.random.permutation(jax.random.fold_in(own, 3), number_of)
    source_of, sink = mixed[0:number_of // 2 * 2:2], mixed[1:number_of // 2 * 2:2]
    margin = jnp.minimum(lengths[source_of] - 1, most - lengths[sink]) // 2
    margin = jnp.where((source_of == order[0]) | (sink == order[0]) | (lengths[sink] == 0), 0, jnp.maximum(margin, 0))
    passed = jax.random.randint(jax.random.fold_in(own, 4), (number_of // 2,), 0, 1 << 20) % (margin + 1)
    lengths = lengths.at[source_of].add(-passed).at[sink].add(passed)
    items = jnp.searchsorted(jnp.cumsum(lengths), jnp.arange(rows * top), side="right").astype(jnp.int32)
    grid = items.reshape(top, rows).T
    grid = grid[jax.random.permutation(jax.random.fold_in(own, 1), rows)]
    turn = jax.random.randint(jax.random.fold_in(own, 2), (rows, 1), 0, top)
    return jnp.take_along_axis(grid, (jnp.arange(top)[None, :] + turn) % top, axis=1)


def portions_of(count, total, limit, lean, full):
    loads = [(1 << 20) // math.isqrt(rank ** lean) + 1 for rank in range(1, count + 1)]
    largest = limit if full else min(limit, max(-(-total // count), total * loads[0] // sum(loads)))
    least = 1 if total - largest >= count - 1 else 0
    given, spare = [largest] + [least] * (count - 1), total - largest - least * (count - 1)
    while spare > 0:
        candidates = [i for i in range(1, count) if given[i] < largest] or [i for i in range(1, count) if given[i] < limit]
        pool, left = sum([loads[i] for i in candidates]), spare
        for i in candidates:
            addition = min(limit - given[i], max(1, left * loads[i] // pool), spare)
            given[i] = given[i] + addition
            spare = spare - addition
    return np.array(given)


def centred(key, dims, width, bound, cuts=(), kind=jnp.bfloat16):
    array = width * jax.random.normal(key, dims, jnp.float32)
    if cuts:
        array = array * level_of(key, dims, cuts, -0.22, 0.18)
    return jnp.clip(array, -bound, bound).astype(kind)


def setup_inputs(seed: int = 0) -> dict:
    key_of = jax.random.split(jax.random.key(seed), 10)
    queries = draw_queries(jax.random.fold_in(key_of[9], 71), 0)
    kv_cache = draw_kv_cache(jax.random.fold_in(key_of[9], 71), 0)
    ctx_len = jax.vmap(lambda own: ragged(own, REQ_DEV, (PAGES_DEV - REQ_DEV) * PAGE, MAXP * PAGE, 2))(jax.random.split(key_of[2], N_INST * N_EP)).reshape((N_INST, N_EP, REQ_DEV)).astype(jnp.int32)
    page_order = jax.vmap(lambda own: jax.random.permutation(own, PAGES_DEV))(jax.random.split(key_of[3], N_INST * N_EP)).reshape((N_INST, N_EP, PAGES_DEV)).astype(jnp.int32)
    hidden_in = centred(key_of[4], (N_INST * N_EP * TOK_DEV, D), 1.0, 6.0, ((0, 256),))
    routes_keys = jax.random.split(jax.random.fold_in(key_of[5], 1), (N_INST * N_EP * TOK_DEV) // TOK_DEV)
    routes_turns = jax.random.permutation(jax.random.fold_in(key_of[5], 3), (N_INST * N_EP * TOK_DEV) // TOK_DEV)
    routes = jax.vmap(lambda own, number: deal_out(jax.random.fold_in(key_of[5], 2), own, number, TOK_DEV, EXPERTS, TOP, CAP, 2))(routes_keys, routes_turns).reshape((N_INST * N_EP * TOK_DEV, TOP))
    w_gate = centred(key_of[6], (N_EP, D, FF // FF_SPLIT), D ** -0.5, 0.09375, ((0, 16),))
    w_up = centred(key_of[7], (N_EP, D, FF // FF_SPLIT), D ** -0.5, 0.09375, ((0, 16),))
    w_down = centred(key_of[8], (N_EP, FF // FF_SPLIT, D), FF ** -0.5, 0.15625, ((0, 16),))
    return {"queries": queries, "kv_cache": kv_cache, "ctx_len": ctx_len, "page_order": page_order, "hidden_in": hidden_in, "routes": routes, "w_gate": w_gate, "w_up": w_up, "w_down": w_down}


def attend(queries, kv_cache, ctx_len, page_order):
    pages = (ctx_len + PAGE - 1) // PAGE
    start = jnp.cumsum(pages) - pages
    slots = jnp.minimum(start[:, None] + jnp.arange(MAXP, dtype=jnp.int32)[None, :], PAGES_DEV - 1).astype(jnp.int32)
    page_of = page_order[slots]
    kv_pages = kv_cache[:, page_of]
    reqs = queries.shape[0]
    group = HEADS // KV_HEADS
    keys = kv_pages[0].reshape(reqs, MAXP * PAGE, KV_HEADS, HEAD_DIM).astype(jnp.float32)
    values = kv_pages[1].reshape(reqs, MAXP * PAGE, KV_HEADS, HEAD_DIM).astype(jnp.float32)
    query = queries.reshape(reqs, KV_HEADS, group, HEAD_DIM).astype(jnp.float32)
    scores = jnp.einsum('rkgd,rtkd->rkgt', query, keys) * (HEAD_DIM ** -0.5)
    inside = (jnp.arange(MAXP * PAGE, dtype=jnp.int32)[None, :] < ctx_len[:, None])[:, None, None, :]
    scores = jnp.where(inside, scores, -1e30)
    top = jnp.max(scores, axis=-1, keepdims=True)
    expo = jnp.exp(scores - top)
    probs = (expo / jnp.sum(expo, axis=-1, keepdims=True)).astype(jnp.bfloat16)
    mixed = jnp.einsum('rkgt,rtkd->rkgd', probs.astype(jnp.float32), values)
    attn = mixed.reshape(reqs, HEADS * HEAD_DIM).astype(jnp.bfloat16)
    keep = (jnp.arange(MAXP, dtype=jnp.int32) < pages[0])[None, :, None, None]
    moved = jnp.where(keep, kv_pages[:, 0], jnp.zeros_like(kv_pages[:, 0]))
    return attn, moved


def expert_part(rows, gate_w, up_w, down_w):
    gate = jnp.dot(rows, gate_w, preferred_element_type=jnp.float32)
    upper = jnp.dot(rows, up_w, preferred_element_type=jnp.float32)
    hidden = (jax.nn.silu(gate) * upper).astype(jnp.bfloat16)
    return jnp.dot(hidden, down_w, preferred_element_type=jnp.float32).astype(jnp.bfloat16)


def instance_moe(packed):
    tokens, expert, w_gate, w_up, w_down = packed
    tokens = tokens.reshape(N_EP, TOK_DEV, D)
    expert = expert.reshape(N_EP, TOK_DEV)
    match = (expert[:, :, None] == jnp.arange(EXPERTS, dtype=jnp.int32)[None, None, :]).astype(jnp.int32)
    rank = jnp.cumsum(match, axis=1) - match
    slot = jnp.sum(rank * match, axis=-1)
    target = expert * CAP + slot
    onehot = (target[:, None, :] == jnp.arange(EXPERTS * CAP, dtype=jnp.int32)[None, :, None]).astype(jnp.float32)
    buffer = jnp.einsum('sct,std->scd', onehot, tokens.astype(jnp.float32)).astype(jnp.bfloat16)
    buffer = buffer.reshape(N_EP, EXPERTS, CAP, D)

    def quarter(item):
        index, gate_w, up_w, down_w = item
        rows = lax.dynamic_index_in_dim(buffer, index // FF_SPLIT, 1, keepdims=False)
        return expert_part(rows.reshape(N_EP * CAP, D), gate_w, up_w, down_w).reshape(N_EP, CAP, D)

    parts = lax.map(quarter, (jnp.arange(N_EP, dtype=jnp.int32), w_gate, w_up, w_down))
    summed = parts.astype(jnp.float32).reshape(EXPERTS, FF_SPLIT, N_EP, CAP, D).sum(axis=1)
    source = jnp.arange(N_EP, dtype=jnp.int32)[:, None] + jnp.zeros((1, TOK_DEV), jnp.int32)
    picked = summed[expert, source, slot]
    return picked.reshape(N_EP * TOK_DEV, D).astype(jnp.bfloat16)


def reference(queries, kv_cache, ctx_len, page_order, hidden_in, routes, w_gate, w_up, w_down):
    per_device = jax.vmap(attend)
    attn_out, moved_all = lax.map(lambda item: per_device(*item), (queries, kv_cache, ctx_len, page_order))
    half = N_INST // 2
    moved_pages = jnp.concatenate([jnp.zeros_like(moved_all[:half]), moved_all[:N_INST - half]], axis=0)
    tokens = hidden_in.reshape(N_INST, N_EP * TOK_DEV, D)
    expert = routes[:, 0].reshape(N_INST, N_EP * TOK_DEV)
    moe_out = lax.map(lambda item: instance_moe((item[0], item[1], w_gate, w_up, w_down)), (tokens, expert))
    return attn_out, moe_out.reshape(N_INST * N_EP * TOK_DEV, D), moved_pages
```

```python
import jax
import jax.numpy as jnp
from jax import lax
from jax.sharding import PartitionSpec as P

HEADS = 64
KV_HEADS = 4
HEAD_DIM = 128
PAGE = 64
MAXP = 8
CAP = 64
HALF = 32
NX, NY, NZ, NC = 4, 4, 8, 2


def device_id(x, y, z, c):
    x, y, z = x % NX, y % NY, z % NZ
    return ((z // 2) * NY + y) * 16 + x * 4 + (z % 2) * 2 + c


def shifted(block, dx=0, dz=0, dc=0):
    route = [
        (device_id(x, y, z, c), device_id(x + dx, y, z + dz, c ^ dc))
        for x in range(NX)
        for y in range(NY)
        for z in range(NZ)
        for c in range(NC)
    ]
    return lax.ppermute(block, ("inst", "ep"), route)


def gather_pages(kv_cache, ctx_len, page_order):
    pages = (ctx_len + PAGE - 1) // PAGE
    start = jnp.cumsum(pages) - pages
    slots = jnp.minimum(
        start[:, None] + jnp.arange(MAXP, dtype=jnp.int32)[None, :], page_order.shape[0] - 1
    )
    return kv_cache[:, page_order[slots]], pages


def attend(queries, kv_pages, ctx_len):
    reqs = queries.shape[0]
    group = HEADS // KV_HEADS
    keys = kv_pages[0].reshape(reqs, MAXP * PAGE, KV_HEADS, HEAD_DIM)
    values = kv_pages[1].reshape(reqs, MAXP * PAGE, KV_HEADS, HEAD_DIM)
    query = queries.reshape(reqs, KV_HEADS, group, HEAD_DIM)
    scores = jnp.einsum(
        "rkgd,rtkd->rkgt", query, keys, preferred_element_type=jnp.float32
    ) * HEAD_DIM ** (-0.5)
    inside = (jnp.arange(MAXP * PAGE, dtype=jnp.int32)[None, :] < ctx_len[:, None])[
        :, None, None, :
    ]
    scores = jnp.where(inside, scores, -1e30)
    top = jnp.max(scores, axis=-1, keepdims=True)
    expo = jnp.exp(scores - top)
    probs = (expo / jnp.sum(expo, axis=-1, keepdims=True)).astype(jnp.bfloat16)
    mixed = jnp.einsum("rkgt,rtkd->rkgd", probs, values, preferred_element_type=jnp.float32)
    return mixed.reshape(reqs, HEADS * HEAD_DIM).astype(jnp.bfloat16)


def expert_part(rows, gate_w, up_w, down_w):
    gate = jnp.dot(rows, gate_w, preferred_element_type=jnp.float32)
    upper = jnp.dot(rows, up_w, preferred_element_type=jnp.float32)
    hidden = (jax.nn.silu(gate) * upper).astype(jnp.bfloat16)
    return jnp.dot(hidden, down_w, preferred_element_type=jnp.float32).astype(jnp.bfloat16)


def add(a, b):
    return (a.astype(jnp.float32) + b.astype(jnp.float32)).astype(jnp.bfloat16)


def spread(pieces):
    size = CAP * len(pieces)
    own = pieces[0] if len(pieces) == 1 else jnp.concatenate(pieces, 0)
    above = shifted(own[: size // 2], dz=1)
    below = shifted(own[size // 2 :], dz=-1)
    mine = jnp.concatenate([own, above, below], 0)
    return jnp.concatenate([mine, shifted(mine, dc=1)], 0)


def collect(part):
    size = part.shape[0] // 4
    mine = add(part[: 2 * size], shifted(part[2 * size :], dc=1))
    first = shifted(mine[size : size + size // 2], dz=-1)
    second = shifted(mine[size + size // 2 :], dz=1)
    own = add(mine[:size], jnp.concatenate([first, second], 0))
    return [own[i : i + CAP] for i in range(0, size, CAP)]


def local(queries, kv_cache, ctx_len, page_order, hidden_in, routes, w_gate, w_up, w_down):
    lengths = ctx_len[0, 0]
    kv_pages, pages = gather_pages(kv_cache[0, 0], lengths, page_order[0, 0])
    keep = (jnp.arange(MAXP, dtype=jnp.int32) < pages[0])[None, :, None, None]
    leaving = jnp.where(keep, kv_pages[:, 0], jnp.zeros_like(kv_pages[:, 0]))
    arrived = lax.ppermute(leaving, "inst", [(i, i + 8) for i in range(8)])
    attn_out = attend(queries[0, 0], kv_pages, lengths)

    x = lax.axis_index("ep") // 4
    weights = (w_gate[0], w_up[0], w_down[0])
    rel = jnp.bitwise_and(routes[:, 0] - x, 3)
    match = (rel[:, None] == jnp.arange(NX, dtype=jnp.int32)[None, :]).astype(jnp.int32)
    rank = jnp.cumsum(match, axis=0) - match
    slot = jnp.sum(rank * match, axis=1)
    target = rel * CAP + slot
    onehot = (target[None, :] == jnp.arange(NX * CAP, dtype=jnp.int32)[:, None]).astype(
        jnp.bfloat16
    )
    buffer = jnp.dot(onehot, hidden_in, preferred_element_type=jnp.float32).astype(jnp.bfloat16)
    piece = [buffer[i * CAP : (i + 1) * CAP] for i in range(NX)]
    got = [piece[0]] + [shifted(piece[d], dx=d) for d in (1, 3, 2)]
    groups = [[got[0]], [got[1], got[2]], [got[3]]]
    back = []
    for g in groups:
        back += collect(expert_part(spread(g), *weights))
    home = [back[0], shifted(back[1], dx=-1), shifted(back[3], dx=-2), shifted(back[2], dx=-3)]
    moe_out = lax.dot_general(
        onehot,
        jnp.concatenate(home, 0),
        (((0,), (0,)), ((), ())),
        preferred_element_type=jnp.float32,
    ).astype(jnp.bfloat16)
    return attn_out[None, None], moe_out, arrived[None, None]


def solution(mesh):
    placed = (
        P("inst", "ep", None, None),
        P("inst", "ep", None, None, None, None),
        P("inst", "ep", None),
        P("inst", "ep", None),
        P(("inst", "ep"), None),
        P(("inst", "ep"), None),
        P("ep", None, None),
        P("ep", None, None),
        P("ep", None, None),
    )
    return jax.shard_map(
        local,
        mesh=mesh,
        in_specs=placed,
        out_specs=(
            P("inst", "ep", None, None),
            P(("inst", "ep"), None),
            P("inst", "ep", None, None, None, None),
        ),
        check_vma=False,
    )
```

```python
import functools

import jax
import jax.numpy as jnp
from jax import lax
from jax.experimental import pallas as pl
from jax.experimental.pallas import tpu as pltpu
from jax.sharding import PartitionSpec as P

HEADS = 64
KV_HEADS = 4
HEAD_DIM = 128
GROUP = HEADS // KV_HEADS
PAGE = 64
MAXP = 8
PAGES = 16
REQS = 4
CAP = 64
TOK = 128
D = 4096
FQ = 384
NX, NY, NZ, NC = 4, 4, 8, 2
K_STEPS, N_STEPS = 4, 4
MIB = 1 << 20
VMEM = pltpu.VMEM
SMEM = pltpu.SMEM


def device_id(x, y, z, c):
    x, y, z = x % NX, y % NY, z % NZ
    return ((z // 2) * NY + y) * 16 + x * 4 + (z % 2) * 2 + c


def move(block, to):
    route = [
        (device_id(x, y, z, c), device_id(*to(x, y, z, c)))
        for x in range(NX)
        for y in range(NY)
        for z in range(NZ)
        for c in range(NC)
    ]
    return lax.ppermute(block, ("inst", "ep"), route)


def over_x(block, dx):
    return move(block, lambda x, y, z, c: (x + dx, y, z, c))


def over_z(block):
    return move(block, lambda x, y, z, c: (x, y, z + 1 - 2 * c, c))


def back_over_z(block):
    return move(block, lambda x, y, z, c: (x, y, z - 1 + 2 * c, c))


def other_core(block):
    return move(block, lambda x, y, z, c: (x, y, z, 1 - c))


def pack_kernel(routes, hidden, onehot, *pieces):
    x = lax.axis_index("ep") // 4
    rel = jnp.bitwise_and(routes[...] - x, NX - 1)
    match = (rel == lax.broadcasted_iota(jnp.int32, (8, TOK), 0)).astype(jnp.float32)
    earlier = lax.broadcasted_iota(jnp.int32, (TOK, TOK), 0) < lax.broadcasted_iota(
        jnp.int32, (TOK, TOK), 1
    )
    rank = jnp.dot(
        match.astype(jnp.bfloat16),
        earlier.astype(jnp.float32).astype(jnp.bfloat16),
        preferred_element_type=jnp.float32,
    )
    slot = jnp.sum(rank * match, axis=0, keepdims=True).astype(jnp.int32)
    target = rel * CAP + slot
    chosen = (lax.broadcasted_iota(jnp.int32, (NX * CAP, TOK), 0) == target).astype(jnp.float32)
    onehot[...] = chosen.astype(jnp.bfloat16)
    for d in (2, 1, 3, 0):
        pieces[d][...] = jnp.dot(
            onehot[d * CAP : (d + 1) * CAP, :], hidden[...], preferred_element_type=jnp.float32
        ).astype(jnp.bfloat16)


def pack(routes, hidden):
    return pl.pallas_call(
        pack_kernel,
        out_shape=[jax.ShapeDtypeStruct((NX * CAP, TOK), jnp.bfloat16)]
        + [jax.ShapeDtypeStruct((CAP, D), jnp.bfloat16)] * NX,
        in_specs=[pl.BlockSpec(memory_space=VMEM)] * 2,
        out_specs=[pl.BlockSpec(memory_space=VMEM)] * (1 + NX),
        compiler_params=pltpu.CompilerParams(vmem_limit_bytes=12 * MIB),
        cost_estimate=pl.CostEstimate(
            flops=2 * NX * CAP * TOK * D, bytes_accessed=3 * MIB, transcendentals=0
        ),
        name="pack",
    )(routes.reshape(1, TOK), hidden)


def leave_kernel(ctx, order, kv, out):
    pages = (ctx[0] + (PAGE - 1)) // PAGE
    for j in range(MAXP):
        page = kv[:, order[j]]
        out[:, j] = jnp.where(j < pages, page, jnp.zeros_like(page))


def leave(ctx, order, kv):
    return pl.pallas_call(
        leave_kernel,
        out_shape=jax.ShapeDtypeStruct((2, MAXP, PAGE, KV_HEADS * HEAD_DIM), jnp.bfloat16),
        in_specs=[pl.BlockSpec(memory_space=SMEM)] * 2 + [pl.BlockSpec(memory_space=VMEM)],
        out_specs=pl.BlockSpec(memory_space=VMEM),
        compiler_params=pltpu.CompilerParams(vmem_limit_bytes=8 * MIB),
        cost_estimate=pl.CostEstimate(flops=0, bytes_accessed=3 * MIB, transcendentals=0),
        name="leave",
    )(ctx, order, kv)


def attend_kernel(ctx, order, queries, kv, out):
    start = 0
    for r in range(REQS):
        length = ctx[r]
        page_of = [order[jnp.minimum(start + j, PAGES - 1)] for j in range(MAXP)]
        start = start + (length + (PAGE - 1)) // PAGE
        inside = lax.broadcasted_iota(jnp.int32, (GROUP, MAXP * PAGE), 1) < length
        for g in range(KV_HEADS):
            cols = slice(g * HEAD_DIM, (g + 1) * HEAD_DIM)
            keys = jnp.concatenate([kv[0, p, :, cols] for p in page_of], 0)
            values = jnp.concatenate([kv[1, p, :, cols] for p in page_of], 0)
            scores = lax.dot_general(
                queries[r, g * GROUP : (g + 1) * GROUP, :],
                keys,
                (((1,), (1,)), ((), ())),
                preferred_element_type=jnp.float32,
            ) * HEAD_DIM ** (-0.5)
            scores = jnp.where(inside, scores, -1e30)
            expo = jnp.exp(scores - jnp.max(scores, axis=-1, keepdims=True))
            probs = (expo / jnp.sum(expo, axis=-1, keepdims=True)).astype(jnp.bfloat16)
            out[r, g * GROUP : (g + 1) * GROUP, :] = jnp.dot(
                probs, values, preferred_element_type=jnp.float32
            ).astype(jnp.bfloat16)


def attend(ctx, order, queries, kv):
    out = pl.pallas_call(
        attend_kernel,
        out_shape=jax.ShapeDtypeStruct((REQS, HEADS, HEAD_DIM), jnp.bfloat16),
        in_specs=[pl.BlockSpec(memory_space=SMEM)] * 2 + [pl.BlockSpec(memory_space=VMEM)] * 2,
        out_specs=pl.BlockSpec(memory_space=VMEM),
        compiler_params=pltpu.CompilerParams(vmem_limit_bytes=10 * MIB),
        cost_estimate=pl.CostEstimate(
            flops=4 * REQS * HEADS * MAXP * PAGE * HEAD_DIM,
            bytes_accessed=2 * MIB,
            transcendentals=REQS * HEADS * MAXP * PAGE,
        ),
        name="attend",
    )(ctx, order, queries.reshape(REQS, HEADS, HEAD_DIM), kv)
    return out.reshape(REQS, HEADS * HEAD_DIM)


def expert_kernel(count, *refs):
    rows, refs = refs[:count], refs[count:]
    gates, ups, downs, refs = refs[:2], refs[2:4], refs[4:6], refs[6:]
    outs, (gate, upper, hidden) = refs[:count], refs[count:]
    step = pl.program_id(0)

    @pl.when(step < K_STEPS)
    def _():
        block = jnp.concatenate([r[...] for r in rows], 0)
        new_gate = jnp.dot(
            block,
            jnp.concatenate([w[...] for w in gates], 1),
            preferred_element_type=jnp.float32,
        )
        new_upper = jnp.dot(
            block,
            jnp.concatenate([w[...] for w in ups], 1),
            preferred_element_type=jnp.float32,
        )

        @pl.when(step == 0)
        def _():
            gate[...] = new_gate
            upper[...] = new_upper

        @pl.when(step > 0)
        def _():
            gate[...] += new_gate
            upper[...] += new_upper

    @pl.when(step == K_STEPS - 1)
    def _():
        v = gate[...]
        hidden[...] = (v / (1.0 + jnp.exp(-v)) * upper[...]).astype(jnp.bfloat16)

    @pl.when(step >= K_STEPS)
    def _():
        part = jnp.dot(
            hidden[...],
            jnp.concatenate([w[...] for w in downs], 0),
            preferred_element_type=jnp.float32,
        ).astype(jnp.bfloat16)
        for i, out in enumerate(outs):
            out[...] = part[i * CAP : (i + 1) * CAP]


def experts(rows, gates, ups, downs):
    count = len(rows)
    size = count * CAP
    kb, nb = D // K_STEPS, D // N_STEPS

    def early(i):
        return jnp.minimum(i, K_STEPS - 1)

    def late(i):
        return jnp.maximum(i - K_STEPS, 0)

    return pl.pallas_call(
        functools.partial(expert_kernel, count),
        out_shape=[jax.ShapeDtypeStruct((CAP, D), jnp.bfloat16)] * count,
        grid=(K_STEPS + N_STEPS,),
        in_specs=[pl.BlockSpec((CAP, kb), lambda i: (0, early(i)))] * count
        + [pl.BlockSpec((kb, FQ), lambda i: (early(i), 0))] * 4
        + [pl.BlockSpec((FQ, nb), lambda i: (0, late(i)))] * 2,
        out_specs=[pl.BlockSpec((CAP, nb), lambda i: (0, late(i)))] * count,
        scratch_shapes=[
            pltpu.VMEM((size, 2 * FQ), jnp.float32),
            pltpu.VMEM((size, 2 * FQ), jnp.float32),
            pltpu.VMEM((size, 2 * FQ), jnp.bfloat16),
        ],
        compiler_params=pltpu.CompilerParams(vmem_limit_bytes=24 * MIB),
        cost_estimate=pl.CostEstimate(
            flops=12 * size * D * FQ, bytes_accessed=18 * MIB, transcendentals=0
        ),
        name="experts",
    )(*rows, *gates, *ups, *downs)


def home_kernel(onehot, *refs):
    *pieces, out = refs
    out[...] = lax.dot_general(
        onehot[...],
        jnp.concatenate([p[...] for p in pieces], 0),
        (((0,), (0,)), ((), ())),
        preferred_element_type=jnp.float32,
    ).astype(jnp.bfloat16)


def bring_home(onehot, pieces):
    nb = D // 4
    return pl.pallas_call(
        home_kernel,
        out_shape=jax.ShapeDtypeStruct((TOK, D), jnp.bfloat16),
        grid=(4,),
        in_specs=[pl.BlockSpec((NX * CAP, TOK), lambda i: (0, 0))]
        + [pl.BlockSpec((CAP, nb), lambda i: (0, i))] * NX,
        out_specs=pl.BlockSpec((TOK, nb), lambda i: (0, i)),
        compiler_params=pltpu.CompilerParams(vmem_limit_bytes=12 * MIB),
        cost_estimate=pl.CostEstimate(
            flops=2 * NX * CAP * TOK * D, bytes_accessed=3 * MIB, transcendentals=0
        ),
        name="bring_home",
    )(onehot, *pieces)


def add(a, b):
    return (a.astype(jnp.float32) + b.astype(jnp.float32)).astype(jnp.bfloat16)


def local(queries, kv_cache, ctx_len, page_order, hidden_in, routes, w_gate, w_up, w_down):
    ctx, order, kv = ctx_len[0, 0], page_order[0, 0], kv_cache[0, 0]
    onehot, *piece = pack(routes, hidden_in)
    got = [piece[0]] + [over_x(piece[d], d) for d in (1, 2, 3)]
    arrived = lax.ppermute(leave(ctx, order, kv), "inst", [(i, i + 8) for i in range(8)])
    gates, ups, downs = ((w[0], other_core(w[0])) for w in (w_gate, w_up, w_down))
    attn_out = attend(ctx, order, queries[0, 0], kv)
    across = [over_z(g) for g in got]
    home = [None] * NX
    for group in ((0, 1, 3), (2,)):
        rows = [got[d] for d in group] + [across[d] for d in group]
        part = experts(rows, gates, ups, downs)
        for i, d in enumerate(group):
            whole = add(part[i], back_over_z(part[len(group) + i]))
            home[d] = over_x(whole, -d) if d else whole
    moe_out = bring_home(onehot, home)
    return attn_out[None, None], moe_out, arrived[None, None]


def solution(mesh):
    placed = (
        P("inst", "ep", None, None),
        P("inst", "ep", None, None, None, None),
        P("inst", "ep", None),
        P("inst", "ep", None),
        P(("inst", "ep"), None),
        P(("inst", "ep"), None),
        P("ep", None, None),
        P("ep", None, None),
        P("ep", None, None),
    )
    return jax.shard_map(
        local,
        mesh=mesh,
        in_specs=placed,
        out_specs=(
            P("inst", "ep", None, None),
            P(("inst", "ep"), None),
            P("inst", "ep", None, None, None, None),
        ),
        check_vma=False,
    )
```

```python
import functools

import jax
import jax.numpy as jnp
from jax import lax
from jax.experimental import pallas as pl
from jax.experimental.pallas import tpu as pltpu
from jax.sharding import PartitionSpec as P

HEADS = 64
KV_HEADS = 4
HEAD_DIM = 128
GROUP = HEADS // KV_HEADS
PAGE = 64
MAXP = 8
PAGES = 16
REQS = 4
CAP = 64
TOK = 128
D = 4096
FQ = 384
NX, NY, NZ, NC = 4, 4, 8, 2
KB, NB = 2048, 1024
EARLY = 4
MIB = 1 << 20
VMEM = pltpu.VMEM
SMEM = pltpu.SMEM
LANE = 128
NO_COST = pl.CostEstimate(flops=0, bytes_accessed=0, transcendentals=0)
ANYWHERE = [pl.BlockSpec(memory_space=pl.ANY)]


def device_id(x, y, z, c):
    x, y, z = x % NX, y % NY, z % NZ
    return ((z // 2) * NY + y) * 16 + x * 4 + (z % 2) * 2 + c


def move(block, to):
    route = [
        (device_id(x, y, z, c), device_id(*to(x, y, z, c)))
        for x in range(NX)
        for y in range(NY)
        for z in range(NZ)
        for c in range(NC)
    ]
    return lax.ppermute(block, ("inst", "ep"), route)


def over_x(block, dx):
    return move(block, lambda x, y, z, c: (x + dx, y, z, c))


def over_z(block):
    return move(block, lambda x, y, z, c: (x, y, z + 1 - 2 * c, c))


def back_over_z(block):
    return move(block, lambda x, y, z, c: (x, y, z - 1 + 2 * c, c))


def other_core(block):
    return move(block, lambda x, y, z, c: (x, y, z, 1 - c))


def bundle_copies(weights, bundle):
    gate, up, down = weights
    copies, row = [], 0
    for w in (gate, up, down):
        size = w.shape[0]
        for j in range(w.shape[1] // LANE):
            copies.append((w.at[:, j * LANE : (j + 1) * LANE], bundle.at[row : row + size, :]))
            row += size
    return copies


def pack_kernel(routes, hidden, *refs):
    weights, (onehot, *pieces, bundle), (tokens, named, sems) = refs[:3], refs[3:9], refs[9:]
    first = [(routes, named), (hidden, tokens)]
    copies = [
        pltpu.make_async_copy(src, dst, sems.at[i])
        for i, (src, dst) in enumerate(first + bundle_copies(weights, bundle))
    ]
    for copy in copies:
        copy.start()
    copies[0].wait()
    x = lax.axis_index("ep") // 4
    rel = jnp.bitwise_and(named[...] - x, NX - 1)
    match = (rel == lax.broadcasted_iota(jnp.int32, (8, TOK), 0)).astype(jnp.float32)
    earlier = lax.broadcasted_iota(jnp.int32, (TOK, TOK), 0) < lax.broadcasted_iota(
        jnp.int32, (TOK, TOK), 1
    )
    rank = jnp.dot(
        match.astype(jnp.bfloat16),
        earlier.astype(jnp.float32).astype(jnp.bfloat16),
        preferred_element_type=jnp.float32,
    )
    slot = jnp.sum(rank * match, axis=0, keepdims=True).astype(jnp.int32)
    target = rel * CAP + slot
    chosen = (lax.broadcasted_iota(jnp.int32, (NX * CAP, TOK), 0) == target).astype(jnp.float32)
    onehot[...] = chosen.astype(jnp.bfloat16)
    copies[1].wait()
    for d in range(NX):
        pieces[d][...] = jnp.dot(
            onehot[d * CAP : (d + 1) * CAP, :], tokens[...], preferred_element_type=jnp.float32
        ).astype(jnp.bfloat16)
    for copy in copies[2:]:
        copy.wait()


def pack(routes, hidden, gate, up, down):
    return pl.pallas_call(
        pack_kernel,
        out_shape=[jax.ShapeDtypeStruct((NX * CAP, TOK), jnp.bfloat16)]
        + [jax.ShapeDtypeStruct((CAP, D), jnp.bfloat16)] * NX
        + [jax.ShapeDtypeStruct((9 * D, LANE), jnp.bfloat16)],
        in_specs=[pl.BlockSpec(memory_space=pltpu.HBM)] * 5,
        out_specs=[pl.BlockSpec(memory_space=VMEM)] * (2 + NX),
        scratch_shapes=[
            pltpu.VMEM((TOK, D), jnp.bfloat16),
            pltpu.VMEM((1, TOK), jnp.int32),
            pltpu.SemaphoreType.DMA((2 + 6 + D // LANE,)),
        ],
        compiler_params=pltpu.CompilerParams(vmem_limit_bytes=8 * MIB),
        cost_estimate=NO_COST,
        name="pack",
    )(
        *(
            pltpu.with_memory_space_constraint(v, pltpu.HBM)
            for v in (routes.reshape(1, TOK), hidden, gate, up, down)
        )
    )


def leave_kernel(parts, ctx, order, kv, *refs):
    out = refs[-1]
    pages = (ctx[0] + (PAGE - 1)) // PAGE
    for i, (side, j) in enumerate(parts):
        page = kv[side, order[j]]
        out[i] = jnp.where(j < pages, page, jnp.zeros_like(page))


def leave(parts, ctx, order, kv, *deps):
    return pl.pallas_call(
        functools.partial(leave_kernel, parts),
        out_shape=jax.ShapeDtypeStruct((len(parts), PAGE, KV_HEADS * HEAD_DIM), jnp.bfloat16),
        in_specs=[pl.BlockSpec(memory_space=SMEM)] * 2
        + [pl.BlockSpec(memory_space=VMEM)]
        + ANYWHERE * len(deps),
        out_specs=pl.BlockSpec(memory_space=VMEM),
        compiler_params=pltpu.CompilerParams(vmem_limit_bytes=8 * MIB),
        cost_estimate=NO_COST,
        name="leave",
    )(ctx, order, kv, *deps)


def land_kernel(*refs):
    *blocks, out = refs
    row = 0
    for block in blocks:
        out[row : row + block.shape[0]] = block[...]
        row += block.shape[0]


def land(*blocks):
    rows = 2 * MAXP
    out = pl.pallas_call(
        land_kernel,
        out_shape=jax.ShapeDtypeStruct((rows, PAGE, KV_HEADS * HEAD_DIM), jnp.bfloat16),
        in_specs=[pl.BlockSpec(memory_space=VMEM)] * len(blocks),
        out_specs=pl.BlockSpec(memory_space=VMEM),
        compiler_params=pltpu.CompilerParams(vmem_limit_bytes=8 * MIB),
        cost_estimate=NO_COST,
        name="land",
    )(*blocks)
    return out.reshape(2, MAXP, PAGE, KV_HEADS * HEAD_DIM)


def onward(block):
    return lax.ppermute(block, "inst", [(i, i + 8) for i in range(8)])


def attend_kernel(ctx, order, queries, kv, *refs):
    out = refs[-1]
    start = 0
    for r in range(REQS):
        length = ctx[r]
        page_of = [order[jnp.minimum(start + j, PAGES - 1)] for j in range(MAXP)]
        start = start + (length + (PAGE - 1)) // PAGE
        inside = lax.broadcasted_iota(jnp.int32, (GROUP, MAXP * PAGE), 1) < length
        for g in range(KV_HEADS):
            cols = slice(g * HEAD_DIM, (g + 1) * HEAD_DIM)
            keys = jnp.concatenate([kv[0, p, :, cols] for p in page_of], 0)
            values = jnp.concatenate([kv[1, p, :, cols] for p in page_of], 0)
            scores = lax.dot_general(
                queries[r, g * GROUP : (g + 1) * GROUP, :],
                keys,
                (((1,), (1,)), ((), ())),
                preferred_element_type=jnp.float32,
            ) * HEAD_DIM ** (-0.5)
            scores = jnp.where(inside, scores, -1e30)
            expo = jnp.exp(scores - jnp.max(scores, axis=-1, keepdims=True))
            probs = (expo / jnp.sum(expo, axis=-1, keepdims=True)).astype(jnp.bfloat16)
            mixed = jnp.dot(probs, values, preferred_element_type=jnp.float32).astype(jnp.bfloat16)
            for h in range(GROUP):
                head = (g * GROUP + h) * HEAD_DIM
                out[r : r + 1, head : head + HEAD_DIM] = mixed[h : h + 1, :]


def attend(ctx, order, queries, kv, *deps):
    return pl.pallas_call(
        attend_kernel,
        out_shape=jax.ShapeDtypeStruct((REQS, HEADS * HEAD_DIM), jnp.bfloat16),
        in_specs=[pl.BlockSpec(memory_space=SMEM)] * 2
        + [pl.BlockSpec(memory_space=VMEM)] * 2
        + ANYWHERE * len(deps),
        out_specs=pl.BlockSpec(memory_space=VMEM),
        compiler_params=pltpu.CompilerParams(vmem_limit_bytes=8 * MIB),
        cost_estimate=pl.CostEstimate(
            flops=0, bytes_accessed=12 * MIB, transcendentals=0
        ),
        name="attend",
    )(ctx, order, queries.reshape(REQS, HEADS, HEAD_DIM), kv, *deps)


def expert_kernel(*refs):
    rows, bundles, (*outs, gate, upper, hidden) = refs[:2], refs[2:4], refs[-5:]

    def widen(k, first):
        ks = pl.ds(pl.multiple_of(k * KB, KB), KB)
        block = jnp.concatenate([r[:, ks] for r in rows], 0)
        for base, total in ((0, gate), (3 * D, upper)):
            new = jnp.dot(
                block,
                jnp.concatenate(
                    [
                        w[pl.ds(pl.multiple_of(base + j * D + k * KB, KB), KB), :]
                        for w in bundles
                        for j in range(3)
                    ],
                    1,
                ),
                preferred_element_type=jnp.float32,
            )
            if first:
                total[...] = new
            else:
                total[...] += new

    widen(0, True)

    @pl.loop(1, D // KB)
    def _(k):
        widen(k, False)

    v = gate[...]
    hidden[...] = (v / (1.0 + jnp.exp(-v)) * upper[...]).astype(jnp.bfloat16)
    across = NB // LANE

    @pl.loop(0, D // NB)
    def _(n):
        ns = pl.ds(pl.multiple_of(n * NB, NB), NB)
        down = jnp.concatenate(
            [
                jnp.concatenate(
                    [
                        w[pl.ds(pl.multiple_of(6 * D + (n * across + j) * FQ, LANE), FQ), :]
                        for j in range(across)
                    ],
                    1,
                )
                for w in bundles
            ],
            0,
        )
        part = jnp.dot(hidden[...], down, preferred_element_type=jnp.float32).astype(jnp.bfloat16)
        for i, out in enumerate(outs):
            out[:, ns] = part[i * CAP : (i + 1) * CAP]


def experts(rows, bundles, *deps):
    size = 2 * CAP
    return pl.pallas_call(
        expert_kernel,
        out_shape=[jax.ShapeDtypeStruct((CAP, D), jnp.bfloat16)] * 2,
        in_specs=[pl.BlockSpec(memory_space=VMEM)] * 4 + ANYWHERE * len(deps),
        out_specs=[pl.BlockSpec(memory_space=VMEM)] * 2,
        scratch_shapes=[
            pltpu.VMEM((size, 2 * FQ), jnp.float32),
            pltpu.VMEM((size, 2 * FQ), jnp.float32),
            pltpu.VMEM((size, 2 * FQ), jnp.bfloat16),
        ],
        compiler_params=pltpu.CompilerParams(vmem_limit_bytes=8 * MIB),
        cost_estimate=pl.CostEstimate(
            flops=0, bytes_accessed=12 * MIB, transcendentals=0
        ),
        name="experts",
    )(*rows, *bundles, *deps)


def hold_kernel(block, *refs):
    refs[-1][...] = block[...]


def hold(block, *deps):
    return pl.pallas_call(
        hold_kernel,
        out_shape=jax.ShapeDtypeStruct(block.shape, block.dtype),
        in_specs=[pl.BlockSpec(memory_space=VMEM)] + ANYWHERE * len(deps),
        out_specs=pl.BlockSpec(memory_space=VMEM),
        compiler_params=pltpu.CompilerParams(vmem_limit_bytes=8 * MIB),
        cost_estimate=NO_COST,
        name="hold",
    )(block, *deps)


def home_kernel(onehot, *refs):
    *pieces, out = refs
    out[...] = lax.dot_general(
        onehot[...],
        jnp.concatenate([p[...] for p in pieces], 0),
        (((0,), (0,)), ((), ())),
        preferred_element_type=jnp.float32,
    ).astype(jnp.bfloat16)


def bring_home(onehot, pieces):
    nb = D // 4
    return pl.pallas_call(
        home_kernel,
        out_shape=jax.ShapeDtypeStruct((TOK, D), jnp.bfloat16),
        grid=(4,),
        in_specs=[pl.BlockSpec((NX * CAP, TOK), lambda i: (0, 0))]
        + [pl.BlockSpec((CAP, nb), lambda i: (0, i))] * NX,
        out_specs=pl.BlockSpec((TOK, nb), lambda i: (0, i)),
        compiler_params=pltpu.CompilerParams(vmem_limit_bytes=8 * MIB),
        cost_estimate=NO_COST,
        name="bring_home",
    )(onehot, *pieces)


def add_kernel(a, b, out):
    out[...] = (a[...].astype(jnp.float32) + b[...].astype(jnp.float32)).astype(jnp.bfloat16)


def add(a, b):
    return pl.pallas_call(
        add_kernel,
        out_shape=jax.ShapeDtypeStruct(a.shape, a.dtype),
        in_specs=[pl.BlockSpec(memory_space=VMEM)] * 2,
        out_specs=pl.BlockSpec(memory_space=VMEM),
        compiler_params=pltpu.CompilerParams(vmem_limit_bytes=8 * MIB),
        cost_estimate=NO_COST,
        name="add",
    )(a, b)


def local(queries, kv_cache, ctx_len, page_order, hidden_in, routes, w_gate, w_up, w_down):
    ctx, order, kv = ctx_len[0, 0], page_order[0, 0], kv_cache[0, 0]
    leaving = [(side, j) for side in range(2) for j in range(MAXP)]
    onehot, *piece, bundle = pack(routes, hidden_in, w_gate[0], w_up[0], w_down[0])
    bundles = tuple(
        pltpu.with_memory_space_constraint(b, VMEM) for b in (bundle, other_core(bundle))
    )
    first = onward(leave(leaving[:EARLY], ctx, order, kv, onehot))
    attn_out = attend(ctx, order, queries[0, 0], kv, onehot)
    got = [piece[0]] + [over_x(piece[d], d) for d in (1, 2, 3)]
    got[1] = hold(got[1], attn_out, first)
    got[2] = hold(got[2], got[3])
    across = [over_z(g) for g in got]
    home = [None] * NX
    whole = {}
    kept = attn_out
    for d in (1, 3, 2, 0):
        deps = (kept,) if d else (kept, whole[1], whole[3])
        kept, lent = experts((got[d], across[d]), bundles, *deps)
        returned = back_over_z(lent)
        whole[d] = add(kept, returned)
        home[d] = over_x(whole[d], -d) if d else whole[d]
    rest = onward(leave(leaving[EARLY:], ctx, order, kv, returned))
    moe_out = bring_home(onehot, home)
    return attn_out[None, None], moe_out, land(first, rest)[None, None]


def solution(mesh):
    placed = (
        P("inst", "ep", None, None),
        P("inst", "ep", None, None, None, None),
        P("inst", "ep", None),
        P("inst", "ep", None),
        P(("inst", "ep"), None),
        P(("inst", "ep"), None),
        P("ep", None, None),
        P("ep", None, None),
        P("ep", None, None),
    )
    return jax.shard_map(
        local,
        mesh=mesh,
        in_specs=placed,
        out_specs=(
            P("inst", "ep", None, None),
            P(("inst", "ep"), None),
            P("inst", "ep", None, None, None, None),
        ),
        check_vma=False,
    )
```

```python
import functools

import jax
import jax.numpy as jnp
from jax import lax
from jax.experimental import pallas as pl
from jax.experimental.pallas import tpu as pltpu
from jax.sharding import PartitionSpec as P

HEADS = 64
KV_HEADS = 4
HEAD_DIM = 128
GROUP = HEADS // KV_HEADS
PAGE = 64
MAXP = 8
PAGES = 16
REQS = 4
CAP = 64
TOK = 128
D = 4096
FQ = 384
NX, NY, NZ, NC = 4, 4, 8, 2
KB, NB = 2048, 1024
EARLY = 12
MIB = 1 << 20
VMEM = pltpu.VMEM
SMEM = pltpu.SMEM
LANE = 128
EXTRA = 16
NO_COST = pl.CostEstimate(flops=0, bytes_accessed=0, transcendentals=0)
ANYWHERE = [pl.BlockSpec(memory_space=pl.ANY)]


def device_id(x, y, z, c):
    x, y, z = x % NX, y % NY, z % NZ
    return ((z // 2) * NY + y) * 16 + x * 4 + (z % 2) * 2 + c


def move(block, to):
    route = [
        (device_id(x, y, z, c), device_id(*to(x, y, z, c)))
        for x in range(NX)
        for y in range(NY)
        for z in range(NZ)
        for c in range(NC)
    ]
    return lax.ppermute(block, ("inst", "ep"), route)


def over_x(block, dx):
    return move(block, lambda x, y, z, c: (x + dx, y, z, c))


def over_z(block):
    return move(block, lambda x, y, z, c: (x, y, z + 1 - 2 * c, c))


def back_over_z(block):
    return move(block, lambda x, y, z, c: (x, y, z - 1 + 2 * c, c))


def other_core(block):
    return move(block, lambda x, y, z, c: (x, y, z, 1 - c))


def bundle_copies(weights, bundle):
    gate, up, down = weights
    copies, row = [], 0
    for w in (gate, up, down):
        size = w.shape[0]
        for j in range(w.shape[1] // LANE):
            copies.append((w.at[:, j * LANE : (j + 1) * LANE], bundle.at[row : row + size, :]))
            row += size
    return copies


def place(routes, onehot):
    x = lax.axis_index("ep") // 4
    rel = jnp.bitwise_and(routes - x, NX - 1)
    match = (rel == lax.broadcasted_iota(jnp.int32, (8, TOK), 0)).astype(jnp.float32)
    earlier = lax.broadcasted_iota(jnp.int32, (TOK, TOK), 0) < lax.broadcasted_iota(
        jnp.int32, (TOK, TOK), 1
    )
    rank = jnp.dot(
        match.astype(jnp.bfloat16),
        earlier.astype(jnp.float32).astype(jnp.bfloat16),
        preferred_element_type=jnp.float32,
    )
    slot = jnp.sum(rank * match, axis=0, keepdims=True).astype(jnp.int32)
    target = rel * CAP + slot
    chosen = (lax.broadcasted_iota(jnp.int32, (NX * CAP, TOK), 0) == target).astype(jnp.float32)
    onehot[...] = chosen.astype(jnp.bfloat16)


def pick(onehot, tokens, pieces):
    for d in range(NX):
        pieces[d][...] = jnp.dot(
            onehot[d * CAP : (d + 1) * CAP, :], tokens[...], preferred_element_type=jnp.float32
        ).astype(jnp.bfloat16)


def pack_kernel(routes, hidden, *refs):
    weights, (onehot, *pieces, bundle, parcel), (named, sems) = refs[:3], refs[3:10], refs[10:]
    tokens = parcel.at[:TOK, :]
    first = [(routes, named), (hidden, tokens)]
    copies = [
        pltpu.make_async_copy(src, dst, sems.at[i])
        for i, (src, dst) in enumerate(first + bundle_copies(weights, bundle))
    ]
    for copy in copies:
        copy.start()
    copies[0].wait()
    parcel[TOK:, :LANE] = jnp.broadcast_to(
        named[...].astype(jnp.float32), (EXTRA, TOK)
    ).astype(jnp.bfloat16)
    parcel[TOK:, LANE:] = jnp.zeros((EXTRA, D - LANE), jnp.bfloat16)
    place(named[...], onehot)
    copies[1].wait()
    pick(onehot, tokens, pieces)
    for copy in copies[2:]:
        copy.wait()


def pack_other_kernel(parcel, *refs):
    pieces, onehot = refs[-5:-1], refs[-1]
    named = parcel[TOK:, :LANE].astype(jnp.float32)[:1].astype(jnp.int32)
    place(named, onehot)
    pick(onehot, parcel.at[:TOK, :], pieces)


def pack_other(parcel, *deps):
    return pl.pallas_call(
        pack_other_kernel,
        out_shape=[jax.ShapeDtypeStruct((CAP, D), jnp.bfloat16)] * NX,
        in_specs=[pl.BlockSpec(memory_space=VMEM)] + ANYWHERE * len(deps),
        out_specs=[pl.BlockSpec(memory_space=VMEM)] * NX,
        scratch_shapes=[pltpu.VMEM((NX * CAP, TOK), jnp.bfloat16)],
        compiler_params=pltpu.CompilerParams(vmem_limit_bytes=8 * MIB),
        cost_estimate=NO_COST,
        name="pack_other",
    )(parcel, *deps)


def pack(routes, hidden, gate, up, down):
    return pl.pallas_call(
        pack_kernel,
        out_shape=[jax.ShapeDtypeStruct((NX * CAP, TOK), jnp.bfloat16)]
        + [jax.ShapeDtypeStruct((CAP, D), jnp.bfloat16)] * NX
        + [jax.ShapeDtypeStruct((9 * D, LANE), jnp.bfloat16)]
        + [jax.ShapeDtypeStruct((TOK + EXTRA, D), jnp.bfloat16)],
        in_specs=ANYWHERE * 5,
        out_specs=[pl.BlockSpec(memory_space=VMEM)] * (3 + NX),
        scratch_shapes=[
            pltpu.VMEM((1, TOK), jnp.int32),
            pltpu.SemaphoreType.DMA((2 + 6 + D // LANE,)),
        ],
        compiler_params=pltpu.CompilerParams(vmem_limit_bytes=8 * MIB),
        cost_estimate=NO_COST,
        name="pack",
    )(
        *(
            pltpu.with_memory_space_constraint(v, pltpu.HBM)
            for v in (routes.reshape(1, TOK), hidden, gate, up, down)
        )
    )


def leave_kernel(parts, ctx, order, kv, *refs):
    out = refs[-1]
    pages = (ctx[0] + (PAGE - 1)) // PAGE
    for i, (side, j) in enumerate(parts):
        page = kv[side, order[j]]
        out[i] = jnp.where(j < pages, page, jnp.zeros_like(page))


def leave(parts, ctx, order, kv, *deps):
    return pl.pallas_call(
        functools.partial(leave_kernel, parts),
        out_shape=jax.ShapeDtypeStruct((len(parts), PAGE, KV_HEADS * HEAD_DIM), jnp.bfloat16),
        in_specs=[pl.BlockSpec(memory_space=SMEM)] * 2
        + [pl.BlockSpec(memory_space=VMEM)]
        + ANYWHERE * len(deps),
        out_specs=pl.BlockSpec(memory_space=VMEM),
        compiler_params=pltpu.CompilerParams(vmem_limit_bytes=8 * MIB),
        cost_estimate=NO_COST,
        name="leave",
    )(ctx, order, kv, *deps)


def land_kernel(*refs):
    _, *blocks, out = refs
    row = 0
    for block in blocks:
        out[row : row + block.shape[0]] = block[...]
        row += block.shape[0]


def land(dep, *blocks):
    rows = 2 * MAXP
    out = pl.pallas_call(
        land_kernel,
        out_shape=jax.ShapeDtypeStruct((rows, PAGE, KV_HEADS * HEAD_DIM), jnp.bfloat16),
        in_specs=ANYWHERE + [pl.BlockSpec(memory_space=VMEM)] * len(blocks),
        out_specs=pl.BlockSpec(memory_space=VMEM),
        compiler_params=pltpu.CompilerParams(vmem_limit_bytes=8 * MIB),
        cost_estimate=NO_COST,
        name="land",
    )(dep, *blocks)
    return out.reshape(2, MAXP, PAGE, KV_HEADS * HEAD_DIM)


def onward(block):
    return lax.ppermute(block, "inst", [(i, i + 8) for i in range(8)])


def attend_kernel(ctx, order, queries, kv, *refs):
    out, token = refs[-2:]
    token[...] = jnp.zeros_like(token)
    start = 0
    for r in range(REQS):
        length = ctx[r]
        page_of = [order[jnp.minimum(start + j, PAGES - 1)] for j in range(MAXP)]
        start = start + (length + (PAGE - 1)) // PAGE
        inside = lax.broadcasted_iota(jnp.int32, (GROUP, MAXP * PAGE), 1) < length
        for g in range(KV_HEADS):
            cols = slice(g * HEAD_DIM, (g + 1) * HEAD_DIM)
            keys = jnp.concatenate([kv[0, p, :, cols] for p in page_of], 0)
            values = jnp.concatenate([kv[1, p, :, cols] for p in page_of], 0)
            scores = lax.dot_general(
                queries[r, g * GROUP : (g + 1) * GROUP, :],
                keys,
                (((1,), (1,)), ((), ())),
                preferred_element_type=jnp.float32,
            ) * HEAD_DIM ** (-0.5)
            scores = jnp.where(inside, scores, -1e30)
            expo = jnp.exp(scores - jnp.max(scores, axis=-1, keepdims=True))
            probs = (expo / jnp.sum(expo, axis=-1, keepdims=True)).astype(jnp.bfloat16)
            mixed = jnp.dot(probs, values, preferred_element_type=jnp.float32).astype(jnp.bfloat16)
            for h in range(GROUP):
                head = (g * GROUP + h) * HEAD_DIM
                out[r : r + 1, head : head + HEAD_DIM] = mixed[h : h + 1, :]


def attend(ctx, order, queries, kv, *deps):
    return pl.pallas_call(
        attend_kernel,
        out_shape=[
            jax.ShapeDtypeStruct((REQS, HEADS * HEAD_DIM), jnp.bfloat16),
            jax.ShapeDtypeStruct((8, LANE), jnp.float32),
        ],
        in_specs=[pl.BlockSpec(memory_space=SMEM)] * 2
        + [pl.BlockSpec(memory_space=VMEM)] * 2
        + ANYWHERE * len(deps),
        out_specs=[pl.BlockSpec(memory_space=VMEM)] * 2,
        compiler_params=pltpu.CompilerParams(vmem_limit_bytes=8 * MIB),
        cost_estimate=pl.CostEstimate(
            flops=8 * 10**9, bytes_accessed=12 * MIB, transcendentals=0
        ),
        name="attend",
    )(ctx, order, queries.reshape(REQS, HEADS, HEAD_DIM), kv, *deps)


def expert_kernel(*refs):
    rows, bundles, (*outs, gate, upper, hidden) = refs[:2], refs[2:4], refs[-5:]

    def widen(k, first):
        ks = pl.ds(pl.multiple_of(k * KB, KB), KB)
        block = jnp.concatenate([r[:, ks] for r in rows], 0)
        for base, total in ((0, gate), (3 * D, upper)):
            new = jnp.dot(
                block,
                jnp.concatenate(
                    [
                        w[pl.ds(pl.multiple_of(base + j * D + k * KB, KB), KB), :]
                        for w in bundles
                        for j in range(3)
                    ],
                    1,
                ),
                preferred_element_type=jnp.float32,
            )
            if first:
                total[...] = new
            else:
                total[...] += new

    widen(0, True)

    @pl.loop(1, D // KB)
    def _(k):
        widen(k, False)

    v = gate[...]
    hidden[...] = (v / (1.0 + jnp.exp(-v)) * upper[...]).astype(jnp.bfloat16)
    across = NB // LANE

    @pl.loop(0, D // NB)
    def _(n):
        ns = pl.ds(pl.multiple_of(n * NB, NB), NB)
        down = jnp.concatenate(
            [
                jnp.concatenate(
                    [
                        w[pl.ds(pl.multiple_of(6 * D + (n * across + j) * FQ, LANE), FQ), :]
                        for j in range(across)
                    ],
                    1,
                )
                for w in bundles
            ],
            0,
        )
        part = jnp.dot(hidden[...], down, preferred_element_type=jnp.float32).astype(jnp.bfloat16)
        for i, out in enumerate(outs):
            out[:, ns] = part[i * CAP : (i + 1) * CAP]


def experts(rows, bundles, *deps):
    size = 2 * CAP
    return pl.pallas_call(
        expert_kernel,
        out_shape=[jax.ShapeDtypeStruct((CAP, D), jnp.bfloat16)] * 2,
        in_specs=[pl.BlockSpec(memory_space=VMEM)] * 4 + ANYWHERE * len(deps),
        out_specs=[pl.BlockSpec(memory_space=VMEM)] * 2,
        scratch_shapes=[
            pltpu.VMEM((size, 2 * FQ), jnp.float32),
            pltpu.VMEM((size, 2 * FQ), jnp.float32),
            pltpu.VMEM((size, 2 * FQ), jnp.bfloat16),
        ],
        compiler_params=pltpu.CompilerParams(vmem_limit_bytes=8 * MIB),
        cost_estimate=pl.CostEstimate(
            flops=0, bytes_accessed=12 * MIB, transcendentals=0
        ),
        name="experts",
    )(*rows, *bundles, *deps)


def hold_kernel(block, *refs):
    refs[-1][...] = block[...]


def hold(block, *deps):
    return pl.pallas_call(
        hold_kernel,
        out_shape=jax.ShapeDtypeStruct(block.shape, block.dtype),
        in_specs=[pl.BlockSpec(memory_space=VMEM)] + ANYWHERE * len(deps),
        out_specs=pl.BlockSpec(memory_space=VMEM),
        compiler_params=pltpu.CompilerParams(vmem_limit_bytes=8 * MIB),
        cost_estimate=NO_COST,
        name="hold",
    )(block, *deps)


def home_kernel(onehot, *refs):
    *pieces, out, token = refs
    token[...] = jnp.zeros_like(token)
    out[...] = lax.dot_general(
        onehot[...],
        jnp.concatenate([p[...] for p in pieces], 0),
        (((0,), (0,)), ((), ())),
        preferred_element_type=jnp.float32,
    ).astype(jnp.bfloat16)


def bring_home(onehot, pieces):
    nb = D // 4
    return pl.pallas_call(
        home_kernel,
        out_shape=[
            jax.ShapeDtypeStruct((TOK, D), jnp.bfloat16),
            jax.ShapeDtypeStruct((8, LANE), jnp.float32),
        ],
        grid=(4,),
        in_specs=[pl.BlockSpec((NX * CAP, TOK), lambda i: (0, 0))]
        + [pl.BlockSpec((CAP, nb), lambda i: (0, i))] * NX,
        out_specs=[
            pl.BlockSpec((TOK, nb), lambda i: (0, i)),
            pl.BlockSpec((8, LANE), lambda i: (0, 0)),
        ],
        compiler_params=pltpu.CompilerParams(vmem_limit_bytes=8 * MIB),
        cost_estimate=NO_COST,
        name="bring_home",
    )(onehot, *pieces)


def add_kernel(a, b, *refs):
    refs[-1][...] = (a[...].astype(jnp.float32) + b[...].astype(jnp.float32)).astype(jnp.bfloat16)


def add(a, b, *deps):
    return pl.pallas_call(
        add_kernel,
        out_shape=jax.ShapeDtypeStruct(a.shape, a.dtype),
        in_specs=[pl.BlockSpec(memory_space=VMEM)] * 2 + ANYWHERE * len(deps),
        out_specs=pl.BlockSpec(memory_space=VMEM),
        compiler_params=pltpu.CompilerParams(vmem_limit_bytes=8 * MIB),
        cost_estimate=NO_COST,
        name="add",
    )(a, b, *deps)


def local(queries, kv_cache, ctx_len, page_order, hidden_in, routes, w_gate, w_up, w_down):
    ctx, order, kv = ctx_len[0, 0], page_order[0, 0], kv_cache[0, 0]
    leaving = [(side, j) for side in range(2) for j in range(MAXP)]
    onehot, *piece, bundle, parcel = pack(routes, hidden_in, w_gate[0], w_up[0], w_down[0])
    bundles = tuple(
        pltpu.with_memory_space_constraint(b, VMEM) for b in (bundle, other_core(bundle))
    )
    attn_out, attended = attend(ctx, order, queries[0, 0], kv, onehot)
    their_parcel = over_z(parcel)
    piece[2] = hold(piece[2], their_parcel, attended)
    got = [piece[0]] + [over_x(piece[d], d) for d in (1, 2, 3)]
    theirs = pack_other(their_parcel, attended, got[1], got[3])
    first = onward(leave(leaving[:EARLY], ctx, order, kv, theirs[0]))
    across = [theirs[0]] + [over_x(theirs[d], d) for d in (1, 2, 3)]
    home, whole, kept = {}, {}, {}
    deps = {1: (2,), 3: (1,), 0: (3,)}
    for d in (2, 1, 3, 0):
        need = [kept[i] for i in deps.get(d, ())]
        if d == 1:
            need += [first, across[3]]
        if d == 0:
            need += [whole[2]]
        kept[d], lent = experts((got[d], across[d]), bundles, *need)
        whole[d] = add(kept[d], back_over_z(lent))
        home[d] = over_x(whole[d], -d) if d else whole[d]
    rest = onward(leave(leaving[EARLY:], ctx, order, kv, first))
    moe_out, finished = bring_home(onehot, [home[d] for d in range(NX)])
    return attn_out[None, None], moe_out, land(finished, first, rest)[None, None]


def solution(mesh):
    placed = (
        P("inst", "ep", None, None),
        P("inst", "ep", None, None, None, None),
        P("inst", "ep", None),
        P("inst", "ep", None),
        P(("inst", "ep"), None),
        P(("inst", "ep"), None),
        P("ep", None, None),
        P("ep", None, None),
        P("ep", None, None),
    )
    return jax.shard_map(
        local,
        mesh=mesh,
        in_specs=placed,
        out_specs=(
            P("inst", "ep", None, None),
            P(("inst", "ep"), None),
            P("inst", "ep", None, None, None, None),
        ),
        check_vma=False,
    )
```

```python
import functools

import jax
import jax.numpy as jnp
from jax import lax
from jax.experimental import pallas as pl
from jax.experimental.pallas import tpu as pltpu
from jax.sharding import PartitionSpec as P

HEADS = 64
KV_HEADS = 4
HEAD_DIM = 128
GROUP = HEADS // KV_HEADS
PAGE = 64
MAXP = 8
PAGES = 16
REQS = 4
CAP = 64
TOK = 128
D = 4096
FQ = 384
NX, NY, NZ, NC = 4, 4, 8, 2
KB, NB = 2048, 1024
EARLY = 12
MIB = 1 << 20
VMEM = pltpu.VMEM
SMEM = pltpu.SMEM
LANE = 128
EXTRA = 16
NO_COST = pl.CostEstimate(flops=0, bytes_accessed=0, transcendentals=0)
ANYWHERE = [pl.BlockSpec(memory_space=pl.ANY)]


def device_id(x, y, z, c):
    x, y, z = x % NX, y % NY, z % NZ
    return ((z // 2) * NY + y) * 16 + x * 4 + (z % 2) * 2 + c


def move(block, to):
    route = [
        (device_id(x, y, z, c), device_id(*to(x, y, z, c)))
        for x in range(NX)
        for y in range(NY)
        for z in range(NZ)
        for c in range(NC)
    ]
    return lax.ppermute(block, ("inst", "ep"), route)


def over_x(block, dx):
    return move(block, lambda x, y, z, c: (x + dx, y, z, c))


def over_z(block):
    return move(block, lambda x, y, z, c: (x, y, z + 1 - 2 * c, c))


def back_over_z(block):
    return move(block, lambda x, y, z, c: (x, y, z - 1 + 2 * c, c))


def other_core(block):
    return move(block, lambda x, y, z, c: (x, y, z, 1 - c))


def bundle_copies(weights, bundle):
    gate, up, down = weights
    copies, row = [], 0
    for w in (gate, up, down):
        size = w.shape[0]
        for j in range(w.shape[1] // LANE):
            copies.append((w.at[:, j * LANE : (j + 1) * LANE], bundle.at[row : row + size, :]))
            row += size
    return copies


def place(routes, onehot):
    x = lax.axis_index("ep") // 4
    rel = jnp.bitwise_and(routes - x, NX - 1)
    match = (rel == lax.broadcasted_iota(jnp.int32, (8, TOK), 0)).astype(jnp.float32)
    earlier = lax.broadcasted_iota(jnp.int32, (TOK, TOK), 0) < lax.broadcasted_iota(
        jnp.int32, (TOK, TOK), 1
    )
    rank = jnp.dot(
        match.astype(jnp.bfloat16),
        earlier.astype(jnp.float32).astype(jnp.bfloat16),
        preferred_element_type=jnp.float32,
    )
    slot = jnp.sum(rank * match, axis=0, keepdims=True).astype(jnp.int32)
    target = rel * CAP + slot
    chosen = (lax.broadcasted_iota(jnp.int32, (NX * CAP, TOK), 0) == target).astype(jnp.float32)
    onehot[...] = chosen.astype(jnp.bfloat16)


def pick(onehot, tokens, pieces):
    for d in range(NX):
        pieces[d][...] = jnp.dot(
            onehot[d * CAP : (d + 1) * CAP, :], tokens[...], preferred_element_type=jnp.float32
        ).astype(jnp.bfloat16)


def pack_kernel(routes, hidden, *refs):
    weights, (onehot, *pieces, bundle, parcel), (named, sems) = refs[:3], refs[3:10], refs[10:]
    tokens = parcel.at[:TOK, :]
    first = [(routes, named), (hidden, tokens)]
    copies = [
        pltpu.make_async_copy(src, dst, sems.at[i])
        for i, (src, dst) in enumerate(first + bundle_copies(weights, bundle))
    ]
    for copy in copies:
        copy.start()
    copies[0].wait()
    parcel[TOK:, :LANE] = jnp.broadcast_to(
        named[...].astype(jnp.float32), (EXTRA, TOK)
    ).astype(jnp.bfloat16)
    parcel[TOK:, LANE:] = jnp.zeros((EXTRA, D - LANE), jnp.bfloat16)
    place(named[...], onehot)
    copies[1].wait()
    pick(onehot, tokens, pieces)
    for copy in copies[2:]:
        copy.wait()


def pack_other_kernel(parcel, *refs):
    pieces, onehot = refs[-5:-1], refs[-1]
    named = parcel[TOK:, :LANE].astype(jnp.float32)[:1].astype(jnp.int32)
    place(named, onehot)
    pick(onehot, parcel.at[:TOK, :], pieces)


def pack_other(parcel, *deps):
    return pl.pallas_call(
        pack_other_kernel,
        out_shape=[jax.ShapeDtypeStruct((CAP, D), jnp.bfloat16)] * NX,
        in_specs=[pl.BlockSpec(memory_space=VMEM)] + ANYWHERE * len(deps),
        out_specs=[pl.BlockSpec(memory_space=VMEM)] * NX,
        scratch_shapes=[pltpu.VMEM((NX * CAP, TOK), jnp.bfloat16)],
        compiler_params=pltpu.CompilerParams(vmem_limit_bytes=8 * MIB),
        cost_estimate=NO_COST,
        name="pack_other",
    )(parcel, *deps)


def pack(routes, hidden, gate, up, down):
    return pl.pallas_call(
        pack_kernel,
        out_shape=[jax.ShapeDtypeStruct((NX * CAP, TOK), jnp.bfloat16)]
        + [jax.ShapeDtypeStruct((CAP, D), jnp.bfloat16)] * NX
        + [jax.ShapeDtypeStruct((9 * D, LANE), jnp.bfloat16)]
        + [jax.ShapeDtypeStruct((TOK + EXTRA, D), jnp.bfloat16)],
        in_specs=ANYWHERE * 5,
        out_specs=[pl.BlockSpec(memory_space=VMEM)] * (3 + NX),
        scratch_shapes=[
            pltpu.VMEM((1, TOK), jnp.int32),
            pltpu.SemaphoreType.DMA((2 + 6 + D // LANE,)),
        ],
        compiler_params=pltpu.CompilerParams(vmem_limit_bytes=8 * MIB),
        cost_estimate=NO_COST,
        name="pack",
    )(
        *(
            pltpu.with_memory_space_constraint(v, pltpu.HBM)
            for v in (routes.reshape(1, TOK), hidden, gate, up, down)
        )
    )


def leave_kernel(parts, ctx, order, kv, *refs):
    out = refs[-1]
    pages = (ctx[0] + (PAGE - 1)) // PAGE
    for i, (side, j) in enumerate(parts):
        page = kv[side, order[j]]
        out[i] = jnp.where(j < pages, page, jnp.zeros_like(page))


def leave(parts, ctx, order, kv, *deps):
    return pl.pallas_call(
        functools.partial(leave_kernel, parts),
        out_shape=jax.ShapeDtypeStruct((len(parts), PAGE, KV_HEADS * HEAD_DIM), jnp.bfloat16),
        in_specs=[pl.BlockSpec(memory_space=SMEM)] * 2
        + [pl.BlockSpec(memory_space=VMEM)]
        + ANYWHERE * len(deps),
        out_specs=pl.BlockSpec(memory_space=VMEM),
        compiler_params=pltpu.CompilerParams(vmem_limit_bytes=8 * MIB),
        cost_estimate=NO_COST,
        name="leave",
    )(ctx, order, kv, *deps)


def land_kernel(*refs):
    _, *blocks, out = refs
    row = 0
    for block in blocks:
        out[row : row + block.shape[0]] = block[...]
        row += block.shape[0]


def land(dep, *blocks):
    rows = 2 * MAXP
    out = pl.pallas_call(
        land_kernel,
        out_shape=jax.ShapeDtypeStruct((rows, PAGE, KV_HEADS * HEAD_DIM), jnp.bfloat16),
        in_specs=ANYWHERE + [pl.BlockSpec(memory_space=VMEM)] * len(blocks),
        out_specs=pl.BlockSpec(memory_space=VMEM),
        compiler_params=pltpu.CompilerParams(vmem_limit_bytes=8 * MIB),
        cost_estimate=NO_COST,
        name="land",
    )(dep, *blocks)
    return out.reshape(2, MAXP, PAGE, KV_HEADS * HEAD_DIM)


def onward(block):
    return lax.ppermute(block, "inst", [(i, i + 8) for i in range(8)])


def attend_kernel(ctx, order, queries, kv, *refs):
    out, token = refs[-2:]
    token[...] = jnp.zeros_like(token)
    start = 0
    for r in range(REQS):
        length = ctx[r]
        page_of = [order[jnp.minimum(start + j, PAGES - 1)] for j in range(MAXP)]
        start = start + (length + (PAGE - 1)) // PAGE
        inside = lax.broadcasted_iota(jnp.int32, (GROUP, MAXP * PAGE), 1) < length
        for g in range(KV_HEADS):
            cols = slice(g * HEAD_DIM, (g + 1) * HEAD_DIM)
            keys = jnp.concatenate([kv[0, p, :, cols] for p in page_of], 0)
            values = jnp.concatenate([kv[1, p, :, cols] for p in page_of], 0)
            scores = lax.dot_general(
                queries[r, g * GROUP : (g + 1) * GROUP, :],
                keys,
                (((1,), (1,)), ((), ())),
                preferred_element_type=jnp.float32,
            ) * HEAD_DIM ** (-0.5)
            scores = jnp.where(inside, scores, -1e30)
            expo = jnp.exp(scores - jnp.max(scores, axis=-1, keepdims=True))
            probs = (expo / jnp.sum(expo, axis=-1, keepdims=True)).astype(jnp.bfloat16)
            mixed = jnp.dot(probs, values, preferred_element_type=jnp.float32).astype(jnp.bfloat16)
            for h in range(GROUP):
                head = (g * GROUP + h) * HEAD_DIM
                out[r : r + 1, head : head + HEAD_DIM] = mixed[h : h + 1, :]


def attend(ctx, order, queries, kv, *deps):
    return pl.pallas_call(
        attend_kernel,
        out_shape=[
            jax.ShapeDtypeStruct((REQS, HEADS * HEAD_DIM), jnp.bfloat16),
            jax.ShapeDtypeStruct((8, LANE), jnp.float32),
        ],
        in_specs=[pl.BlockSpec(memory_space=SMEM)] * 2
        + [pl.BlockSpec(memory_space=VMEM)] * 2
        + ANYWHERE * len(deps),
        out_specs=[pl.BlockSpec(memory_space=VMEM)] * 2,
        compiler_params=pltpu.CompilerParams(vmem_limit_bytes=8 * MIB),
        cost_estimate=pl.CostEstimate(
            flops=8 * 10**9, bytes_accessed=12 * MIB, transcendentals=0
        ),
        name="attend",
    )(ctx, order, queries.reshape(REQS, HEADS, HEAD_DIM), kv, *deps)


def expert_kernel(*refs):
    rows, bundles, (*outs, gate, upper, hidden) = refs[:2], refs[2:4], refs[-5:]

    def widen(k, first):
        ks = pl.ds(pl.multiple_of(k * KB, KB), KB)
        block = jnp.concatenate([r[:, ks] for r in rows], 0)
        for base, total in ((0, gate), (3 * D, upper)):
            new = jnp.dot(
                block,
                jnp.concatenate(
                    [
                        w[pl.ds(pl.multiple_of(base + j * D + k * KB, KB), KB), :]
                        for w in bundles
                        for j in range(3)
                    ],
                    1,
                ),
                preferred_element_type=jnp.float32,
            )
            if first:
                total[...] = new
            else:
                total[...] += new

    widen(0, True)

    @pl.loop(1, D // KB)
    def _(k):
        widen(k, False)

    v = gate[...]
    hidden[...] = (v / (1.0 + jnp.exp(-v)) * upper[...]).astype(jnp.bfloat16)
    across = NB // LANE

    @pl.loop(0, D // NB)
    def _(n):
        ns = pl.ds(pl.multiple_of(n * NB, NB), NB)
        down = jnp.concatenate(
            [
                jnp.concatenate(
                    [
                        w[pl.ds(pl.multiple_of(6 * D + (n * across + j) * FQ, LANE), FQ), :]
                        for j in range(across)
                    ],
                    1,
                )
                for w in bundles
            ],
            0,
        )
        part = jnp.dot(hidden[...], down, preferred_element_type=jnp.float32).astype(jnp.bfloat16)
        for i, out in enumerate(outs):
            out[:, ns] = part[i * CAP : (i + 1) * CAP]


def experts(rows, bundles, *deps):
    size = 2 * CAP
    return pl.pallas_call(
        expert_kernel,
        out_shape=[jax.ShapeDtypeStruct((CAP, D), jnp.bfloat16)] * 2,
        in_specs=[pl.BlockSpec(memory_space=VMEM)] * 4 + ANYWHERE * len(deps),
        out_specs=[pl.BlockSpec(memory_space=VMEM)] * 2,
        scratch_shapes=[
            pltpu.VMEM((size, 2 * FQ), jnp.float32),
            pltpu.VMEM((size, 2 * FQ), jnp.float32),
            pltpu.VMEM((size, 2 * FQ), jnp.bfloat16),
        ],
        compiler_params=pltpu.CompilerParams(vmem_limit_bytes=8 * MIB),
        cost_estimate=pl.CostEstimate(
            flops=0, bytes_accessed=12 * MIB, transcendentals=0
        ),
        name="experts",
    )(*rows, *bundles, *deps)


def hold_kernel(block, *refs):
    refs[-1][...] = block[...]


def hold(block, *deps):
    return pl.pallas_call(
        hold_kernel,
        out_shape=jax.ShapeDtypeStruct(block.shape, block.dtype),
        in_specs=[pl.BlockSpec(memory_space=VMEM)] + ANYWHERE * len(deps),
        out_specs=pl.BlockSpec(memory_space=VMEM),
        compiler_params=pltpu.CompilerParams(vmem_limit_bytes=8 * MIB),
        cost_estimate=NO_COST,
        name="hold",
    )(block, *deps)


def home_kernel(onehot, *refs):
    *pieces, out, token = refs
    token[...] = jnp.zeros_like(token)
    out[...] = lax.dot_general(
        onehot[...],
        jnp.concatenate([p[...] for p in pieces], 0),
        (((0,), (0,)), ((), ())),
        preferred_element_type=jnp.float32,
    ).astype(jnp.bfloat16)


def bring_home(onehot, pieces):
    nb = D // 4
    return pl.pallas_call(
        home_kernel,
        out_shape=[
            jax.ShapeDtypeStruct((TOK, D), jnp.bfloat16),
            jax.ShapeDtypeStruct((8, LANE), jnp.float32),
        ],
        grid=(4,),
        in_specs=[pl.BlockSpec((NX * CAP, TOK), lambda i: (0, 0))]
        + [pl.BlockSpec((CAP, nb), lambda i: (0, i))] * NX,
        out_specs=[
            pl.BlockSpec((TOK, nb), lambda i: (0, i)),
            pl.BlockSpec((8, LANE), lambda i: (0, 0)),
        ],
        compiler_params=pltpu.CompilerParams(vmem_limit_bytes=8 * MIB),
        cost_estimate=NO_COST,
        name="bring_home",
    )(onehot, *pieces)


def add_kernel(a, b, *refs):
    refs[-1][...] = (a[...].astype(jnp.float32) + b[...].astype(jnp.float32)).astype(jnp.bfloat16)


def add(a, b, *deps):
    return pl.pallas_call(
        add_kernel,
        out_shape=jax.ShapeDtypeStruct(a.shape, a.dtype),
        in_specs=[pl.BlockSpec(memory_space=VMEM)] * 2 + ANYWHERE * len(deps),
        out_specs=pl.BlockSpec(memory_space=VMEM),
        compiler_params=pltpu.CompilerParams(vmem_limit_bytes=8 * MIB),
        cost_estimate=NO_COST,
        name="add",
    )(a, b, *deps)


def local(queries, kv_cache, ctx_len, page_order, hidden_in, routes, w_gate, w_up, w_down):
    ctx, order, kv = ctx_len[0, 0], page_order[0, 0], kv_cache[0, 0]
    leaving = [(side, j) for side in range(2) for j in range(MAXP)]
    onehot, *piece, bundle, parcel = pack(routes, hidden_in, w_gate[0], w_up[0], w_down[0])
    bundles = tuple(
        pltpu.with_memory_space_constraint(b, VMEM) for b in (bundle, other_core(bundle))
    )
    attn_out, attended = attend(ctx, order, queries[0, 0], kv, onehot)
    their_parcel = over_z(parcel)
    got = [piece[0], over_x(piece[1], 1), None, over_x(piece[3], 3)]
    piece[2] = hold(piece[2], got[1], got[3], attended)
    got[2] = over_x(piece[2], 2)
    theirs = pack_other(their_parcel, attended, got[1], got[3])
    first = onward(leave(leaving[:EARLY], ctx, order, kv, theirs[0]))
    across = [theirs[0]] + [over_x(theirs[d], d) for d in (1, 2, 3)]
    home, whole, kept = {}, {}, {}
    deps = {1: (2,), 3: (1,), 0: (3,)}
    for d in (2, 1, 3, 0):
        need = [kept[i] for i in deps.get(d, ())]
        if d == 1:
            need += [first, across[3]]
        if d == 0:
            need += [whole[2]]
        kept[d], lent = experts((got[d], across[d]), bundles, *need)
        whole[d] = add(kept[d], back_over_z(lent))
        home[d] = over_x(whole[d], -d) if d else whole[d]
    rest = onward(leave(leaving[EARLY:], ctx, order, kv, first))
    moe_out, finished = bring_home(onehot, [home[d] for d in range(NX)])
    return attn_out[None, None], moe_out, land(finished, first, rest)[None, None]


def solution(mesh):
    placed = (
        P("inst", "ep", None, None),
        P("inst", "ep", None, None, None, None),
        P("inst", "ep", None),
        P("inst", "ep", None),
        P(("inst", "ep"), None),
        P(("inst", "ep"), None),
        P("ep", None, None),
        P("ep", None, None),
        P("ep", None, None),
    )
    return jax.shard_map(
        local,
        mesh=mesh,
        in_specs=placed,
        out_specs=(
            P("inst", "ep", None, None),
            P(("inst", "ep"), None),
            P("inst", "ep", None, None, None, None),
        ),
        check_vma=False,
    )
```

```python
import functools

import jax
import jax.numpy as jnp
from jax import lax
from jax.experimental import pallas as pl
from jax.experimental.pallas import tpu as pltpu
from jax.sharding import PartitionSpec as P

HEADS = 64
KV_HEADS = 4
HEAD_DIM = 128
GROUP = HEADS // KV_HEADS
PAGE = 64
MAXP = 8
PAGES = 16
REQS = 4
CAP = 64
TOK = 128
D = 4096
FQ = 384
NX, NY, NZ, NC = 4, 4, 8, 2
KB, NB = 2048, 1024
EARLY = 11
MIB = 1 << 20
VMEM = pltpu.VMEM
SMEM = pltpu.SMEM
LANE = 128
EXTRA = 16
NO_COST = pl.CostEstimate(flops=0, bytes_accessed=0, transcendentals=0)
ANYWHERE = [pl.BlockSpec(memory_space=pl.ANY)]


def device_id(x, y, z, c):
    x, y, z = x % NX, y % NY, z % NZ
    return ((z // 2) * NY + y) * 16 + x * 4 + (z % 2) * 2 + c


def move(block, to):
    route = [
        (device_id(x, y, z, c), device_id(*to(x, y, z, c)))
        for x in range(NX)
        for y in range(NY)
        for z in range(NZ)
        for c in range(NC)
    ]
    return lax.ppermute(block, ("inst", "ep"), route)


def over_x(block, dx):
    return move(block, lambda x, y, z, c: (x + dx, y, z, c))


def over_z(block):
    return move(block, lambda x, y, z, c: (x, y, z + 1 - 2 * c, c))


def back_over_z(block):
    return move(block, lambda x, y, z, c: (x, y, z - 1 + 2 * c, c))


def other_core(block):
    return move(block, lambda x, y, z, c: (x, y, z, 1 - c))


def bundle_copies(weights, bundle):
    gate, up, down = weights
    copies, row = [], 0
    for w in (gate, up, down):
        size = w.shape[0]
        for j in range(w.shape[1] // LANE):
            copies.append((w.at[:, j * LANE : (j + 1) * LANE], bundle.at[row : row + size, :]))
            row += size
    return copies


def place(routes, onehot):
    x = lax.axis_index("ep") // 4
    rel = jnp.bitwise_and(routes - x, NX - 1)
    match = (rel == lax.broadcasted_iota(jnp.int32, (8, TOK), 0)).astype(jnp.float32)
    earlier = lax.broadcasted_iota(jnp.int32, (TOK, TOK), 0) < lax.broadcasted_iota(
        jnp.int32, (TOK, TOK), 1
    )
    rank = jnp.dot(
        match.astype(jnp.bfloat16),
        earlier.astype(jnp.float32).astype(jnp.bfloat16),
        preferred_element_type=jnp.float32,
    )
    slot = jnp.sum(rank * match, axis=0, keepdims=True).astype(jnp.int32)
    target = rel * CAP + slot
    chosen = (lax.broadcasted_iota(jnp.int32, (NX * CAP, TOK), 0) == target).astype(jnp.float32)
    onehot[...] = chosen.astype(jnp.bfloat16)


def pick(onehot, tokens, pieces):
    for d in range(NX):
        pieces[d][...] = jnp.dot(
            onehot[d * CAP : (d + 1) * CAP, :], tokens[...], preferred_element_type=jnp.float32
        ).astype(jnp.bfloat16)


def pack_kernel(routes, hidden, *refs):
    weights, (onehot, *pieces, bundle, parcel), (named, sems) = refs[:3], refs[3:10], refs[10:]
    tokens = parcel.at[:TOK, :]
    first = [(routes, named), (hidden, tokens)]
    copies = [
        pltpu.make_async_copy(src, dst, sems.at[i])
        for i, (src, dst) in enumerate(first + bundle_copies(weights, bundle))
    ]
    for copy in copies:
        copy.start()
    copies[0].wait()
    parcel[TOK:, :LANE] = jnp.broadcast_to(
        named[...].astype(jnp.float32), (EXTRA, TOK)
    ).astype(jnp.bfloat16)
    parcel[TOK:, LANE:] = jnp.zeros((EXTRA, D - LANE), jnp.bfloat16)
    place(named[...], onehot)
    copies[1].wait()
    pick(onehot, tokens, pieces)
    for copy in copies[2:]:
        copy.wait()


def pack_other_kernel(parcel, *refs):
    pieces, onehot = refs[-5:-1], refs[-1]
    named = parcel[TOK:, :LANE].astype(jnp.float32)[:1].astype(jnp.int32)
    place(named, onehot)
    pick(onehot, parcel.at[:TOK, :], pieces)


def pack_other(parcel, *deps):
    return pl.pallas_call(
        pack_other_kernel,
        out_shape=[jax.ShapeDtypeStruct((CAP, D), jnp.bfloat16)] * NX,
        in_specs=[pl.BlockSpec(memory_space=VMEM)] + ANYWHERE * len(deps),
        out_specs=[pl.BlockSpec(memory_space=VMEM)] * NX,
        scratch_shapes=[pltpu.VMEM((NX * CAP, TOK), jnp.bfloat16)],
        compiler_params=pltpu.CompilerParams(vmem_limit_bytes=8 * MIB),
        cost_estimate=NO_COST,
        name="pack_other",
    )(parcel, *deps)


def pack(routes, hidden, gate, up, down):
    return pl.pallas_call(
        pack_kernel,
        out_shape=[jax.ShapeDtypeStruct((NX * CAP, TOK), jnp.bfloat16)]
        + [jax.ShapeDtypeStruct((CAP, D), jnp.bfloat16)] * NX
        + [jax.ShapeDtypeStruct((9 * D, LANE), jnp.bfloat16)]
        + [jax.ShapeDtypeStruct((TOK + EXTRA, D), jnp.bfloat16)],
        in_specs=ANYWHERE * 5,
        out_specs=[pl.BlockSpec(memory_space=VMEM)] * (3 + NX),
        scratch_shapes=[
            pltpu.VMEM((1, TOK), jnp.int32),
            pltpu.SemaphoreType.DMA((2 + 6 + D // LANE,)),
        ],
        compiler_params=pltpu.CompilerParams(vmem_limit_bytes=8 * MIB),
        cost_estimate=NO_COST,
        name="pack",
    )(
        *(
            pltpu.with_memory_space_constraint(v, pltpu.HBM)
            for v in (routes.reshape(1, TOK), hidden, gate, up, down)
        )
    )


def leave_kernel(parts, ctx, order, kv, *refs):
    out = refs[-1]
    pages = (ctx[0] + (PAGE - 1)) // PAGE
    for i, (side, j) in enumerate(parts):
        page = kv[side, order[j]]
        out[i] = jnp.where(j < pages, page, jnp.zeros_like(page))


def leave(parts, ctx, order, kv, *deps):
    return pl.pallas_call(
        functools.partial(leave_kernel, parts),
        out_shape=jax.ShapeDtypeStruct((len(parts), PAGE, KV_HEADS * HEAD_DIM), jnp.bfloat16),
        in_specs=[pl.BlockSpec(memory_space=SMEM)] * 2
        + [pl.BlockSpec(memory_space=VMEM)]
        + ANYWHERE * len(deps),
        out_specs=pl.BlockSpec(memory_space=VMEM),
        compiler_params=pltpu.CompilerParams(vmem_limit_bytes=8 * MIB),
        cost_estimate=NO_COST,
        name="leave",
    )(ctx, order, kv, *deps)


def land_kernel(*refs):
    _, *blocks, out = refs
    row = 0
    for block in blocks:
        out[row : row + block.shape[0]] = block[...]
        row += block.shape[0]


def land(dep, *blocks):
    rows = 2 * MAXP
    out = pl.pallas_call(
        land_kernel,
        out_shape=jax.ShapeDtypeStruct((rows, PAGE, KV_HEADS * HEAD_DIM), jnp.bfloat16),
        in_specs=ANYWHERE + [pl.BlockSpec(memory_space=VMEM)] * len(blocks),
        out_specs=pl.BlockSpec(memory_space=VMEM),
        compiler_params=pltpu.CompilerParams(vmem_limit_bytes=8 * MIB),
        cost_estimate=NO_COST,
        name="land",
    )(dep, *blocks)
    return out.reshape(2, MAXP, PAGE, KV_HEADS * HEAD_DIM)


def onward(block):
    return lax.ppermute(block, "inst", [(i, i + 8) for i in range(8)])


def attend_kernel(ctx, order, queries, kv, *refs):
    out, token = refs[-2:]
    token[...] = jnp.zeros_like(token)
    start = 0
    for r in range(REQS):
        length = ctx[r]
        page_of = [order[jnp.minimum(start + j, PAGES - 1)] for j in range(MAXP)]
        start = start + (length + (PAGE - 1)) // PAGE
        inside = lax.broadcasted_iota(jnp.int32, (GROUP, MAXP * PAGE), 1) < length
        for g in range(KV_HEADS):
            cols = slice(g * HEAD_DIM, (g + 1) * HEAD_DIM)
            keys = jnp.concatenate([kv[0, p, :, cols] for p in page_of], 0)
            values = jnp.concatenate([kv[1, p, :, cols] for p in page_of], 0)
            scores = lax.dot_general(
                queries[r, g * GROUP : (g + 1) * GROUP, :],
                keys,
                (((1,), (1,)), ((), ())),
                preferred_element_type=jnp.float32,
            ) * HEAD_DIM ** (-0.5)
            scores = jnp.where(inside, scores, -1e30)
            expo = jnp.exp(scores - jnp.max(scores, axis=-1, keepdims=True))
            probs = (expo / jnp.sum(expo, axis=-1, keepdims=True)).astype(jnp.bfloat16)
            mixed = jnp.dot(probs, values, preferred_element_type=jnp.float32).astype(jnp.bfloat16)
            for h in range(GROUP):
                head = (g * GROUP + h) * HEAD_DIM
                out[r : r + 1, head : head + HEAD_DIM] = mixed[h : h + 1, :]


def attend(ctx, order, queries, kv, *deps):
    return pl.pallas_call(
        attend_kernel,
        out_shape=[
            jax.ShapeDtypeStruct((REQS, HEADS * HEAD_DIM), jnp.bfloat16),
            jax.ShapeDtypeStruct((8, LANE), jnp.float32),
        ],
        in_specs=[pl.BlockSpec(memory_space=SMEM)] * 2
        + [pl.BlockSpec(memory_space=VMEM)] * 2
        + ANYWHERE * len(deps),
        out_specs=[pl.BlockSpec(memory_space=VMEM)] * 2,
        compiler_params=pltpu.CompilerParams(vmem_limit_bytes=8 * MIB),
        cost_estimate=pl.CostEstimate(
            flops=8 * 10**9, bytes_accessed=12 * MIB, transcendentals=0
        ),
        name="attend",
    )(ctx, order, queries.reshape(REQS, HEADS, HEAD_DIM), kv, *deps)


def expert_kernel(*refs):
    rows, bundles, (*outs, gate, upper, hidden) = refs[:2], refs[2:4], refs[-5:]

    def widen(k, first):
        ks = pl.ds(pl.multiple_of(k * KB, KB), KB)
        block = jnp.concatenate([r[:, ks] for r in rows], 0)
        for base, total in ((0, gate), (3 * D, upper)):
            new = jnp.dot(
                block,
                jnp.concatenate(
                    [
                        w[pl.ds(pl.multiple_of(base + j * D + k * KB, KB), KB), :]
                        for w in bundles
                        for j in range(3)
                    ],
                    1,
                ),
                preferred_element_type=jnp.float32,
            )
            if first:
                total[...] = new
            else:
                total[...] += new

    widen(0, True)

    @pl.loop(1, D // KB)
    def _(k):
        widen(k, False)

    v = gate[...]
    hidden[...] = (v / (1.0 + jnp.exp(-v)) * upper[...]).astype(jnp.bfloat16)
    across = NB // LANE

    @pl.loop(0, D // NB)
    def _(n):
        ns = pl.ds(pl.multiple_of(n * NB, NB), NB)
        down = jnp.concatenate(
            [
                jnp.concatenate(
                    [
                        w[pl.ds(pl.multiple_of(6 * D + (n * across + j) * FQ, LANE), FQ), :]
                        for j in range(across)
                    ],
                    1,
                )
                for w in bundles
            ],
            0,
        )
        part = jnp.dot(hidden[...], down, preferred_element_type=jnp.float32).astype(jnp.bfloat16)
        for i, out in enumerate(outs):
            out[:, ns] = part[i * CAP : (i + 1) * CAP]


def experts(rows, bundles, *deps):
    size = 2 * CAP
    return pl.pallas_call(
        expert_kernel,
        out_shape=[jax.ShapeDtypeStruct((CAP, D), jnp.bfloat16)] * 2,
        in_specs=[pl.BlockSpec(memory_space=VMEM)] * 4 + ANYWHERE * len(deps),
        out_specs=[pl.BlockSpec(memory_space=VMEM)] * 2,
        scratch_shapes=[
            pltpu.VMEM((size, 2 * FQ), jnp.float32),
            pltpu.VMEM((size, 2 * FQ), jnp.float32),
            pltpu.VMEM((size, 2 * FQ), jnp.bfloat16),
        ],
        compiler_params=pltpu.CompilerParams(vmem_limit_bytes=8 * MIB),
        cost_estimate=pl.CostEstimate(
            flops=0, bytes_accessed=12 * MIB, transcendentals=0
        ),
        name="experts",
    )(*rows, *bundles, *deps)


def hold_kernel(block, *refs):
    refs[-1][...] = block[...]


def hold(block, *deps):
    return pl.pallas_call(
        hold_kernel,
        out_shape=jax.ShapeDtypeStruct(block.shape, block.dtype),
        in_specs=[pl.BlockSpec(memory_space=VMEM)] + ANYWHERE * len(deps),
        out_specs=pl.BlockSpec(memory_space=VMEM),
        compiler_params=pltpu.CompilerParams(vmem_limit_bytes=8 * MIB),
        cost_estimate=NO_COST,
        name="hold",
    )(block, *deps)


def home_kernel(onehot, *refs):
    *pieces, out, token = refs
    token[...] = jnp.zeros_like(token)
    out[...] = lax.dot_general(
        onehot[...],
        jnp.concatenate([p[...] for p in pieces], 0),
        (((0,), (0,)), ((), ())),
        preferred_element_type=jnp.float32,
    ).astype(jnp.bfloat16)


def bring_home(onehot, pieces):
    nb = D // 4
    return pl.pallas_call(
        home_kernel,
        out_shape=[
            jax.ShapeDtypeStruct((TOK, D), jnp.bfloat16),
            jax.ShapeDtypeStruct((8, LANE), jnp.float32),
        ],
        grid=(4,),
        in_specs=[pl.BlockSpec((NX * CAP, TOK), lambda i: (0, 0))]
        + [pl.BlockSpec((CAP, nb), lambda i: (0, i))] * NX,
        out_specs=[
            pl.BlockSpec((TOK, nb), lambda i: (0, i)),
            pl.BlockSpec((8, LANE), lambda i: (0, 0)),
        ],
        compiler_params=pltpu.CompilerParams(vmem_limit_bytes=8 * MIB),
        cost_estimate=NO_COST,
        name="bring_home",
    )(onehot, *pieces)


def add_kernel(a, b, *refs):
    refs[-1][...] = (a[...].astype(jnp.float32) + b[...].astype(jnp.float32)).astype(jnp.bfloat16)


def add(a, b, *deps):
    return pl.pallas_call(
        add_kernel,
        out_shape=jax.ShapeDtypeStruct(a.shape, a.dtype),
        in_specs=[pl.BlockSpec(memory_space=VMEM)] * 2 + ANYWHERE * len(deps),
        out_specs=pl.BlockSpec(memory_space=VMEM),
        compiler_params=pltpu.CompilerParams(vmem_limit_bytes=8 * MIB),
        cost_estimate=NO_COST,
        name="add",
    )(a, b, *deps)


def local(queries, kv_cache, ctx_len, page_order, hidden_in, routes, w_gate, w_up, w_down):
    ctx, order, kv = ctx_len[0, 0], page_order[0, 0], kv_cache[0, 0]
    leaving = [(side, j) for side in range(2) for j in range(MAXP)]
    onehot, *piece, bundle, parcel = pack(routes, hidden_in, w_gate[0], w_up[0], w_down[0])
    bundles = tuple(
        pltpu.with_memory_space_constraint(b, VMEM) for b in (bundle, other_core(bundle))
    )
    attn_out, attended = attend(ctx, order, queries[0, 0], kv, onehot)
    their_parcel = over_z(parcel)
    got = [piece[0], over_x(piece[1], 1), None, over_x(piece[3], 3)]
    piece[2] = hold(piece[2], got[1], got[3], attended)
    got[2] = over_x(piece[2], 2)
    theirs = pack_other(their_parcel, attended, got[1], got[3])
    first = onward(leave(leaving[:EARLY], ctx, order, kv, theirs[0]))
    across = [theirs[0]] + [over_x(theirs[d], d) for d in (1, 2, 3)]
    home, whole, kept = {}, {}, {}
    deps = {1: (2,), 3: (1,), 0: (3,)}
    for d in (2, 1, 3, 0):
        need = [kept[i] for i in deps.get(d, ())]
        if d == 1:
            need += [first, across[3]]
        if d == 0:
            need += [whole[2]]
        kept[d], lent = experts((got[d], across[d]), bundles, *need)
        whole[d] = add(kept[d], back_over_z(lent))
        home[d] = over_x(whole[d], -d) if d else whole[d]
    rest = onward(leave(leaving[EARLY:], ctx, order, kv, first))
    moe_out, finished = bring_home(onehot, [home[d] for d in range(NX)])
    return attn_out[None, None], moe_out, land(finished, first, rest)[None, None]


def solution(mesh):
    placed = (
        P("inst", "ep", None, None),
        P("inst", "ep", None, None, None, None),
        P("inst", "ep", None),
        P("inst", "ep", None),
        P(("inst", "ep"), None),
        P(("inst", "ep"), None),
        P("ep", None, None),
        P("ep", None, None),
        P("ep", None, None),
    )
    return jax.shard_map(
        local,
        mesh=mesh,
        in_specs=placed,
        out_specs=(
            P("inst", "ep", None, None),
            P(("inst", "ep"), None),
            P("inst", "ep", None, None, None, None),
        ),
        check_vma=False,
    )
```
